512 devices in a mesh: gx: 16 (over x, y_hi), gy: 32 (over z, y_lo, core).
Axes of the slice: x: 4, y: 8 (y_hi: 4, y_lo: 2; y = y_hi * 2 + y_lo), z: 8, core: 2. Of those that a mesh axis runs over, the one named last changes fastest.
Arguments:
- charge: float32 [16, 32, 256], P('gx', 'gy'), may hold values from -9 to 9
- fraction: float32 [3, 16, 32, 256], P(None, 'gx', 'gy'), may hold values from 0 to 1
- base_cell: int32 [16, 32, 256], P('gx', 'gy'), may hold values from 0 to 2047, as said below
- live_slot: int32 [16, 32, 256], P('gx', 'gy'), may hold values 0 or 1
- force_cot: float32 [3, 16, 32, 256], P(None, 'gx', 'gy'), may hold values from -6 to 6
- potential_cot: float32 [16, 32, 256], P('gx', 'gy'), may hold values from -6 to 6
Outputs:
- forces: float32 [3, 16, 32, 256], P(None, 'gx', 'gy')
- potential: float32 [16, 32, 256], P('gx', 'gy')
- charge_grad: float32 [16, 32, 256], P('gx', 'gy')
The draws below stay inside these ranges and needn't reach their ends.
Inputs may be any that keep to these rules, and one draw needn't show every extreme that they name: `base_cell`: x * 8 * 16 + y * 16 + z for the atom's base cell counted inside its domain, z inside the block of its slot; slot s belongs to block s // 16.
All inputs are finite; a program needn't handle non-finite values. No bound on the sum of `live_slot` on one device may be relied on, other than what follows from the above.
Results may differ from the reference program's by a relative error of at most 0.0003.
Values sent between devices are 32-bit elements; how exact they have to be, the bound alone decides.
No kernel may reach another device: no remote copies, remote signals or barrier semaphores. Data moves between devices by JAX's collectives and lax.ppermute only.
A program may use at most 64 MiB of HBM per device.

```python
import math
import jax
import jax.numpy as jnp

K = 256
BZ = 16
SLOTS = 16
CX = 16
CY = 8
NZB = 16
N_GX = 16
N_GY = 32


def cell_numbers(key):
    return jax.random.randint(jax.random.fold_in(key, 101), (N_GX, N_GY, NZB * SLOTS), 0, CX * CY * BZ).astype(jnp.int32)


def draw_base_cell(key, part):
    return cell_numbers(key)


def draw_charge(key, part):
    cells = cell_numbers(key)
    key = jax.random.fold_in(key, 3)
    return 1.5 * jax.random.truncated_normal(key, -6.0, 6.0, cells.shape, jnp.float32)


def place_ends(values, key, low, largest):
    index_at = [jax.random.randint(jax.random.fold_in(key, axis), (), 0, length) for axis, length in enumerate(values.shape)]
    longest = values.shape.index(max(values.shape))
    neighbour = index_at[:longest] + [(index_at[longest] + 1) % values.shape[longest]] + index_at[longest + 1:]
    return values.at[tuple(index_at)].set(low).at[tuple(neighbour)].set(largest)


def steps_of(rng, extent, shards, least, top_value):
    loudness = 1.0
    for axis_at, shards_of in shards:
        steps = jax.random.uniform(jax.random.fold_in(jax.random.fold_in(rng, 6), axis_at), (shards_of,), jnp.float32, least / len(shards), top_value / len(shards))
        loudness = loudness * jnp.repeat(jnp.exp(steps), extent[axis_at] // shards_of).reshape((-1,) + (1,) * (len(extent) - 1 - axis_at))
    return loudness


def scatter_about(rng, extent, width, most, pieces=(), held_as=jnp.bfloat16):
    array = jax.random.normal(rng, extent, jnp.float32) * width
    if len(pieces) > 0:
        array = steps_of(rng, extent, pieces, -0.22, 0.18) * array
    return jnp.clip(array, min=-most, max=most).astype(held_as)


def setup_inputs(seed: int = 0) -> dict:
    arg_keys = jax.random.split(jax.random.key(seed), 7)
    return {
        "charge": draw_charge(jax.random.fold_in(arg_keys[6], 71), 0),
        "fraction": jnp.clip(1.0 * jax.random.uniform(arg_keys[1], (3, N_GX, N_GY, NZB * SLOTS), jnp.float32) ** steps_of(arg_keys[1], (3, N_GX, N_GY, NZB * SLOTS), ((1, 16), (2, 32)), -0.2, 0.2), 0.0, 1.0),
        "base_cell": draw_base_cell(jax.random.fold_in(arg_keys[6], 71), 0),
        "live_slot": place_ends((jax.random.randint(arg_keys[3], (N_GX, N_GY, NZB * SLOTS), 0, 4) < 3).astype(jnp.int32), jax.random.fold_in(arg_keys[3], 1), 0, 1),
        "force_cot": scatter_about(arg_keys[4], (3, N_GX, N_GY, NZB * SLOTS), 1.0, 6.0, ((1, 16), (2, 32)), jnp.float32),
        "potential_cot": scatter_about(arg_keys[5], (N_GX, N_GY, NZB * SLOTS), 1.0, 6.0, ((0, 16), (1, 32)), jnp.float32),
    }


EWALD_SPLIT = 0.8


def spline_terms(fraction):
    square = fraction * fraction
    cubic_part = square * fraction
    remain = 1.0 - fraction
    weights = (remain * remain * remain / 6.0,
               (3.0 * cubic_part - 6.0 * square + 4.0) / 6.0,
               (-3.0 * cubic_part + 3.0 * square + 3.0 * fraction + 1.0) / 6.0,
               cubic_part / 6.0)
    slopes = (-0.5 * remain * remain,
              (3.0 * square - 4.0 * fraction) / 2.0,
              (-3.0 * square + 2.0 * fraction + 1.0) / 2.0,
              0.5 * square)
    return weights, slopes


def influence(freq_x, freq_y, freq_z, length):
    def folded(frequency):
        nearest = jnp.minimum(frequency, length - frequency).astype(jnp.float32)
        return nearest * nearest

    def modulus(frequency):
        cosine = jnp.cos((2.0 * math.pi / length) * frequency.astype(jnp.float32))
        return 9.0 / ((2.0 + cosine) * (2.0 + cosine))

    total_sq = folded(freq_x) + folded(freq_y) + folded(freq_z)
    safe_sq = jnp.maximum(total_sq, 1.0)
    damping = math.pi * math.pi / (EWALD_SPLIT * EWALD_SPLIT * length * length)
    result_value = jnp.exp(-damping * safe_sq) * modulus(freq_x) * modulus(freq_y) * modulus(freq_z) / (math.pi * length * safe_sq)
    return jnp.where(total_sq > 0.0, result_value, 0.0)


def solve_mesh(flat_mesh):
    mesh_grid = flat_mesh.reshape(K, K, K)
    frequency = jnp.arange(K, dtype=jnp.int32)
    half_freq = jnp.arange(K // 2 + 1, dtype=jnp.int32)
    kernel = influence(frequency[:, None, None], frequency[None, :, None], half_freq[None, None, :], K) * (float(K) ** 3)
    return jnp.fft.irfftn(jnp.fft.rfftn(mesh_grid) * kernel, s=(K, K, K)).reshape(-1)


def outer_three(first_term, second_term, third_term):
    return first_term[:, None, None] * second_term[None, :, None] * third_term[None, None, :]


def reference(charge, fraction, base_cell, live_slot, force_cot, potential_cot):
    width_x = K // N_GX
    width_y = K // N_GY
    slot_count = NZB * SLOTS
    device_x = jnp.arange(N_GX, dtype=jnp.int32)[:, None, None]
    device_y = jnp.arange(N_GY, dtype=jnp.int32)[None, :, None]
    slot_block = (jnp.arange(slot_count, dtype=jnp.int32) // SLOTS)[None, None, :]
    offsets = jnp.arange(4, dtype=jnp.int32)[:, None, None, None]
    cell_x = (device_x * width_x + base_cell // (width_y * BZ) - 1 + offsets) % K
    cell_y = (device_y * width_y + (base_cell // BZ) % width_y - 1 + offsets) % K
    cell_z = (slot_block * BZ + base_cell % BZ - 1 + offsets) % K
    flat_index = (cell_x[:, None, None] * K + cell_y[None, :, None]) * K + cell_z[None, None, :]
    weights_x, slopes_x = spline_terms(fraction[0])
    weights_y, slopes_y = spline_terms(fraction[1])
    weights_z, slopes_z = spline_terms(fraction[2])
    weight_x, slope_x = jnp.stack(weights_x), jnp.stack(slopes_x)
    weight_y, slope_y = jnp.stack(weights_y), jnp.stack(slopes_y)
    weight_z, slope_z = jnp.stack(weights_z), jnp.stack(slopes_z)
    plain_cube = outer_three(weight_x, weight_y, weight_z)
    moved_x = outer_three(slope_x, weight_y, weight_z)
    moved_y = outer_three(weight_x, slope_y, weight_z)
    moved_z = outer_three(weight_x, weight_y, slope_z)
    live_mask = live_slot.astype(jnp.float32)
    live_charge = charge * live_mask
    source_terms = -live_charge * (force_cot[0] * moved_x + force_cot[1] * moved_y + force_cot[2] * moved_z) + live_mask * potential_cot * plain_cube
    flat_all = flat_index.reshape(-1)
    charge_mesh = jnp.zeros((K * K * K,), jnp.float32).at[flat_all].add((live_charge * plain_cube).reshape(-1))
    source_mesh = jnp.zeros((K * K * K,), jnp.float32).at[flat_all].add(source_terms.reshape(-1))
    potential_at = solve_mesh(charge_mesh)[flat_index]
    response_at = solve_mesh(source_mesh)[flat_index]
    mesh_value = jnp.sum(plain_cube * potential_at, axis=(0, 1, 2))
    grad_x = jnp.sum(moved_x * potential_at, axis=(0, 1, 2))
    grad_y = jnp.sum(moved_y * potential_at, axis=(0, 1, 2))
    grad_z = jnp.sum(moved_z * potential_at, axis=(0, 1, 2))
    response = jnp.sum(plain_cube * response_at, axis=(0, 1, 2))
    forces = jnp.stack([-live_charge * grad_x, -live_charge * grad_y, -live_charge * grad_z])
    potential = live_mask * mesh_value
    charge_grad = live_mask * (response - force_cot[0] * grad_x - force_cot[1] * grad_y - force_cot[2] * grad_z)
    return (forces, potential, charge_grad)
```

```python
import math

import jax
import jax.numpy as jnp
import ml_dtypes
import numpy as np
from jax import lax
from jax.experimental import pallas as pl
from jax.experimental.pallas import tpu as pltpu
from jax.sharding import PartitionSpec as P

K = 256
CX = 16
CY = 8
EX = CX + 3
EY = CY + 3
N_GX = 16
N_GY = 32
ATOMS = 256
DEVICES = N_GX * N_GY
LANES = 128

EWALD_SPLIT = 0.8


def cas_table(left, right):
    angles = 2.0 * math.pi / K * (left[:, None] * right[None, :] % K)
    return np.cos(angles) + np.sin(angles)


def split_table(table):
    high = table.astype(np.float32).astype(ml_dtypes.bfloat16)
    low = (table - high.astype(np.float64)).astype(np.float32).astype(ml_dtypes.bfloat16)
    return np.stack([high, low])


def extended_coordinates():
    gx, a = np.meshgrid(np.arange(N_GX), np.arange(EX), indexing="ij")
    ext_x = (gx * CX + a - 1).reshape(-1) % K
    b, gy = np.meshgrid(np.arange(EY), np.arange(N_GY), indexing="ij")
    ext_y = (gy * CY + b - 1).reshape(-1) % K
    return ext_x, ext_y


def influence_factors():
    freq = np.arange(K)
    nearest = np.minimum(freq, K - freq).astype(np.float64)
    damping = math.pi * math.pi / (EWALD_SPLIT * EWALD_SPLIT * K * K)
    cosine = np.cos(2.0 * math.pi / K * freq)
    factor = np.exp(-damping * nearest * nearest) * 9.0 / (2.0 + cosine) ** 2
    return factor.astype(np.float32), (nearest * nearest).astype(np.float32)


def split(value):
    high = value.astype(jnp.bfloat16)
    low = (value - high.astype(jnp.float32)).astype(jnp.bfloat16)
    return high, low


def product(left, right, dims=((1,), (0,))):
    def one(a, b):
        return lax.dot_general(a, b, (dims, ((), ())), preferred_element_type=jnp.float32)

    return one(left[0], right[0]) + (one(left[0], right[1]) + one(left[1], right[0]))


def spline_terms(fraction):
    square = fraction * fraction
    cubic_part = square * fraction
    remain = 1.0 - fraction
    weights = (
        remain * remain * remain * (1.0 / 6.0),
        (3.0 * cubic_part - 6.0 * square + 4.0) * (1.0 / 6.0),
        (-3.0 * cubic_part + 3.0 * square + 3.0 * fraction + 1.0) * (1.0 / 6.0),
        cubic_part * (1.0 / 6.0),
    )
    slopes = (
        -0.5 * remain * remain,
        (3.0 * square - 4.0 * fraction) * 0.5,
        (-3.0 * square + 2.0 * fraction + 1.0) * 0.5,
        0.5 * square,
    )
    return weights, slopes


def banded(first, terms, rows, wrap):
    place = lax.broadcasted_iota(jnp.int32, (rows, ATOMS), 0) - first
    if wrap:
        place = jnp.bitwise_and(place, rows - 1)
    hits = [place == offset for offset in range(4)]

    def table(values):
        out = jnp.zeros((rows, ATOMS), jnp.float32)
        for hit, value in zip(hits, values):
            out = jnp.where(hit, jnp.broadcast_to(value, (rows, ATOMS)), out)
        return out

    return [table(values) for values in terms]


def domain_tables(cells, fraction_ref):
    wx, dx = banded(jnp.right_shift(cells, 7), spline_terms(fraction_ref[0, 0]), 24, False)
    cell_y = jnp.bitwise_and(jnp.right_shift(cells, 4), CY - 1)
    wy, dy = banded(cell_y, spline_terms(fraction_ref[1, 0]), 16, False)
    return wx, dx, wy, dy


def spread_kernel(
    charge, fraction, base_cell, live_slot, force_cot, potential_cot, hartley,
    send, spectral, table_a, table_b, table_c,
):
    live = live_slot[0].astype(jnp.float32)
    live_charge = charge[0] * live
    cells = base_cell[0]
    slot = lax.broadcasted_iota(jnp.int32, (1, ATOMS), 1)
    base_z = jnp.bitwise_and(slot, -16) + jnp.bitwise_and(cells, 15)
    wz, dz = banded(base_z - 1, spline_terms(fraction[2, 0]), K, True)
    hart = (hartley[0], hartley[1])
    zw = split(product(hart, split(wz)))
    zd = split(product(hart, split(dz)))
    spectral[0] = zw[0]
    spectral[1] = zw[1]
    spectral[2] = zd[0]
    spectral[3] = zd[1]

    wx, dx, wy, dy = domain_tables(cells, fraction)
    along_x = -live_charge * force_cot[0, 0]
    along_y = -live_charge * force_cot[1, 0]
    along_z = -live_charge * force_cot[2, 0]
    direct = live * potential_cot[0]
    tail = jnp.zeros((48, ATOMS), jnp.float32)
    for table in (table_a, table_b, table_c):
        table[208:256, :] = tail
    for b in range(EY):
        wyb = wy[b : b + 1]
        dyb = dy[b : b + 1]
        rows = pl.ds(b * EX, 24)
        table_a[rows, :] = wx * (live_charge * wyb)
        table_b[rows, :] = dx * (along_x * wyb) + wx * (along_y * dyb + direct * wyb)
        table_c[rows, :] = wx * (along_z * wyb)
    nt = ((1,), (1,))
    first = product(zw, split(table_a[...]), nt)
    second = product(zw, split(table_b[...]), nt) + product(zd, split(table_c[...]), nt)
    for field, value in enumerate((first, second)):
        for half in range(2):
            send[pl.ds(field * 2 * K + half, K, stride=2), :] = value[
                :, half * LANES : (half + 1) * LANES
            ]


def plane_kernel(
    received, hx, hxt, hy, hyt, row_terms, column_terms, scalar_terms, send, plane, blocks
):
    device = lax.axis_index("gx") * N_GY + lax.axis_index("gy")
    freq_z = lax.rem(device, K)
    plane[:, 256:384] = jnp.zeros((EY * N_GY, LANES), jnp.float32)
    for gx in range(N_GX):
        rows = jnp.concatenate(
            [received[pl.ds(gx * 2 * N_GY + half, N_GY, stride=2), :] for half in range(2)], axis=1
        )
        for b in range(EY):
            plane[b * N_GY : (b + 1) * N_GY, gx * EX : (gx + 1) * EX] = rows[
                :, b * EX : (b + 1) * EX
            ]
    mesh_plane = plane[:, : N_GX * EX]
    half_way = product(split(mesh_plane), (hx[0], hx[1]))
    spectrum = product((hyt[0], hyt[1]), split(half_way))
    total_sq = (column_terms[:, 1:2] + row_terms[1:2, :]) + scalar_terms[1, freq_z]
    factor = column_terms[:, 0:1] * (row_terms[0:1, :] * (scalar_terms[0, freq_z] / (math.pi * K)))
    kernel = jnp.where(total_sq > 0.0, factor / jnp.maximum(total_sq, 1.0), 0.0)
    half_way = product((hy[0], hy[1]), split(spectrum * kernel))
    plane[:, : N_GX * EX] = product(split(half_way), (hxt[0], hxt[1]))
    blocks[:, LANES:] = jnp.zeros((DEVICES, LANES), jnp.float32)
    for b in range(EY):
        rows = plane[b * N_GY : (b + 1) * N_GY, :]
        for gx in range(N_GX):
            blocks[gx * N_GY : (gx + 1) * N_GY, b * EX : (b + 1) * EX] = rows[
                :, gx * EX : (gx + 1) * EX
            ]
    for half in range(2):
        send[pl.ds(half, DEVICES, stride=2), :] = blocks[:, half * LANES : (half + 1) * LANES]


def sample_kernel(
    received, spectral, charge, fraction, base_cell, live_slot, force_cot,
    forces, potential, charge_grad, sample_a, sample_b, sample_c,
):
    def field(index):
        halves = [received[pl.ds(index * 2 * K + half, K, stride=2), :] for half in range(2)]
        return split(jnp.concatenate(halves, axis=1).T)

    zw = (spectral[0], spectral[1])
    zd = (spectral[2], spectral[3])
    first = field(0)
    sample_a[...] = product(first, zw)
    sample_b[...] = product(first, zd)
    sample_c[...] = product(field(1), zw)
    live = live_slot[0].astype(jnp.float32)
    live_charge = charge[0] * live
    wx, dx, wy, dy = domain_tables(base_cell[0], fraction)
    sums = [jnp.zeros((24, ATOMS), jnp.float32) for _ in range(5)]
    for b in range(EY):
        wyb = wy[b : b + 1]
        dyb = dy[b : b + 1]
        rows = pl.ds(b * EX, 24)
        plain = sample_a[rows, :]
        plain_x = wx * plain
        sums[0] = sums[0] + plain_x * wyb
        sums[1] = sums[1] + (dx * plain) * wyb
        sums[2] = sums[2] + plain_x * dyb
        sums[3] = sums[3] + (wx * sample_b[rows, :]) * wyb
        sums[4] = sums[4] + (wx * sample_c[rows, :]) * wyb
    mesh_value, grad_x, grad_y, grad_z, response = [
        jnp.sum(value, axis=0, keepdims=True) for value in sums
    ]
    forces[0, 0] = -live_charge * grad_x
    forces[1, 0] = -live_charge * grad_y
    forces[2, 0] = -live_charge * grad_z
    potential[0] = live * mesh_value
    charge_grad[0] = live * (
        response
        - force_cot[0, 0] * grad_x
        - force_cot[1, 0] * grad_y
        - force_cot[2, 0] * grad_z
    )


def exchange(blocks):
    swapped = lax.all_to_all(
        blocks.reshape(DEVICES, 2, LANES), ("gx", "gy"), split_axis=0, concat_axis=0, tiled=True
    )
    return swapped.reshape(2 * DEVICES, LANES)


def on_device(charge, fraction, base_cell, live_slot, force_cot, potential_cot):
    ext_x, ext_y = extended_coordinates()
    freq = np.arange(K)
    factor, squares = influence_factors()
    terms = np.stack([factor, squares])
    hx = cas_table(ext_x, freq)
    hy = cas_table(ext_y, freq)
    params = pltpu.CompilerParams(vmem_limit_bytes=48 * 1024 * 1024)
    vmem = pl.BlockSpec(memory_space=pltpu.VMEM)
    smem = pl.BlockSpec(memory_space=pltpu.SMEM)
    f32 = jnp.float32
    table = pltpu.VMEM((K, ATOMS), f32)
    message = jax.ShapeDtypeStruct((2 * DEVICES, LANES), f32)

    sent, spectral = pl.pallas_call(
        spread_kernel,
        out_shape=(message, jax.ShapeDtypeStruct((4, K, ATOMS), jnp.bfloat16)),
        in_specs=[vmem] * 7,
        out_specs=(vmem, vmem),
        scratch_shapes=[table, table, table],
        compiler_params=params,
        name="spread",
    )(
        charge, fraction, base_cell, live_slot, force_cot, potential_cot,
        jnp.asarray(split_table(cas_table(freq, freq))),
    )
    received = exchange(sent)
    solved = pl.pallas_call(
        plane_kernel,
        out_shape=message,
        in_specs=[vmem] * 7 + [smem],
        out_specs=vmem,
        scratch_shapes=[pltpu.VMEM((EY * N_GY, 384), f32), pltpu.VMEM((DEVICES, 2 * LANES), f32)],
        compiler_params=params,
        name="plane",
    )(
        received,
        jnp.asarray(split_table(hx)),
        jnp.asarray(split_table(hx.T)),
        jnp.asarray(split_table(hy)),
        jnp.asarray(split_table(hy.T)),
        jnp.asarray(terms),
        jnp.asarray(terms.T),
        jnp.asarray(terms),
    )
    returned = exchange(solved)
    return pl.pallas_call(
        sample_kernel,
        out_shape=(
            jax.ShapeDtypeStruct((3, 1, 1, ATOMS), f32),
            jax.ShapeDtypeStruct((1, 1, ATOMS), f32),
            jax.ShapeDtypeStruct((1, 1, ATOMS), f32),
        ),
        in_specs=[vmem] * 7,
        out_specs=(vmem, vmem, vmem),
        scratch_shapes=[table, table, table],
        compiler_params=params,
        name="sample",
    )(returned, spectral, charge, fraction, base_cell, live_slot, force_cot)


def solution(mesh):
    return jax.shard_map(
        on_device,
        mesh=mesh,
        in_specs=(
            P("gx", "gy", None),
            P(None, "gx", "gy", None),
            P("gx", "gy", None),
            P("gx", "gy", None),
            P(None, "gx", "gy", None),
            P("gx", "gy", None),
        ),
        out_specs=(P(None, "gx", "gy", None), P("gx", "gy", None), P("gx", "gy", None)),
        check_vma=False,
    )
```

```python
import math

import jax
import jax.numpy as jnp
import ml_dtypes
import numpy as np
from jax import lax
from jax.experimental import pallas as pl
from jax.experimental.pallas import tpu as pltpu
from jax.sharding import PartitionSpec as P

K = 256
CX = 16
CY = 8
EX = CX + 3
EY = CY + 3
N_GX = 16
N_GY = 32
ATOMS = 256
DEVICES = N_GX * N_GY
LANES = 128
PAD = 384

EWALD_SPLIT = 0.8


def cas_table(left, right):
    angles = 2.0 * math.pi / K * (left[:, None] * right[None, :] % K)
    return np.cos(angles) + np.sin(angles)


def split_table(table):
    high = table.astype(np.float32).astype(ml_dtypes.bfloat16)
    low = (table - high.astype(np.float64)).astype(np.float32).astype(ml_dtypes.bfloat16)
    return np.stack([high, low])


def plane_coordinates():
    gx, a = np.meshgrid(np.arange(N_GX), np.arange(EX), indexing="ij")
    ext_x = (gx * CX + a - 1).reshape(-1) % K
    m, gy = np.meshgrid(np.arange(CY), np.arange(N_GY), indexing="ij")
    return ext_x, (gy * CY + m).reshape(-1)


def influence_factors():
    freq = np.arange(K)
    nearest = np.minimum(freq, K - freq).astype(np.float64)
    damping = math.pi * math.pi / (EWALD_SPLIT * EWALD_SPLIT * K * K)
    cosine = np.cos(2.0 * math.pi / K * freq)
    factor = np.exp(-damping * nearest * nearest) * 9.0 / (2.0 + cosine) ** 2
    return factor.astype(np.float32), (nearest * nearest).astype(np.float32)


def split(value):
    high = value.astype(jnp.bfloat16)
    low = (value - high.astype(jnp.float32)).astype(jnp.bfloat16)
    return high, low


def product(left, right, dims=((1,), (0,))):
    def one(a, b):
        return lax.dot_general(a, b, (dims, ((), ())), preferred_element_type=jnp.float32)

    return one(left[0], right[0]) + (one(left[0], right[1]) + one(left[1], right[0]))


def spline_terms(fraction):
    square = fraction * fraction
    cubic_part = square * fraction
    remain = 1.0 - fraction
    weights = (
        remain * remain * remain * (1.0 / 6.0),
        (3.0 * cubic_part - 6.0 * square + 4.0) * (1.0 / 6.0),
        (-3.0 * cubic_part + 3.0 * square + 3.0 * fraction + 1.0) * (1.0 / 6.0),
        cubic_part * (1.0 / 6.0),
    )
    slopes = (
        -0.5 * remain * remain,
        (3.0 * square - 4.0 * fraction) * 0.5,
        (-3.0 * square + 2.0 * fraction + 1.0) * 0.5,
        0.5 * square,
    )
    return weights, slopes


def banded(first, terms, rows, wrap):
    place = lax.broadcasted_iota(jnp.int32, (rows, ATOMS), 0) - first
    if wrap:
        place = jnp.bitwise_and(place, rows - 1)
    hits = [place == offset for offset in range(4)]

    def table(values):
        out = jnp.zeros((rows, ATOMS), jnp.float32)
        for hit, value in zip(hits, values):
            out = jnp.where(hit, jnp.broadcast_to(value, (rows, ATOMS)), out)
        return out

    return [table(values) for values in terms]


def domain_tables(cells, fraction_ref):
    wx, dx = banded(jnp.right_shift(cells, 7), spline_terms(fraction_ref[0, 0]), 24, False)
    cell_y = jnp.bitwise_and(jnp.right_shift(cells, 4), CY - 1)
    wy, dy = banded(cell_y, spline_terms(fraction_ref[1, 0]), 16, False)
    return wx, dx, wy, dy


def spread_kernel(
    charge_in, fraction_in, cell_in, live_in, force_in, potential_in, hartley_in,
    hx_in, hyt_in, hy_in, hxt_in, rows_in, columns_in,
    send, spectral, atoms, hx, hyt, hy, hxt, row_terms, column_terms,
    charge, fraction, base_cell, live_slot, force_cot, potential_cot, hartley,
    table_a, table_b, table_c, arrived,
):
    pairs = (
        (cell_in, base_cell),
        (fraction_in, fraction),
        (hartley_in, hartley),
        (charge_in, charge),
        (live_in, live_slot),
        (force_in, force_cot),
        (potential_in, potential_cot),
        (hx_in, hx),
        (hyt_in, hyt),
        (hy_in, hy),
        (hxt_in, hxt),
        (rows_in, row_terms),
        (columns_in, column_terms),
    )
    copies = [
        pltpu.make_async_copy(source, target, arrived.at[index])
        for index, (source, target) in enumerate(pairs)
    ]
    for copy in copies:
        copy.start()
    copies[0].wait()
    copies[1].wait()
    cells = base_cell[0]
    slot = lax.broadcasted_iota(jnp.int32, (1, ATOMS), 1)
    base_z = jnp.bitwise_and(slot, -16) + jnp.bitwise_and(cells, 15)
    wz, dz = banded(base_z - 1, spline_terms(fraction[2, 0]), K, True)
    wx, dx, wy, dy = domain_tables(cells, fraction)
    copies[2].wait()
    hart = (hartley[0], hartley[1])
    zw = split(product(hart, split(wz)))
    zd = split(product(hart, split(dz)))
    for copy in copies[3:7]:
        copy.wait()
    live = live_slot[0].astype(jnp.float32)
    live_charge = charge[0] * live
    along_x = -live_charge * force_cot[0, 0]
    along_y = -live_charge * force_cot[1, 0]
    along_z = -live_charge * force_cot[2, 0]
    direct = live * potential_cot[0]
    tail = jnp.zeros((48, ATOMS), jnp.float32)
    for table in (table_a, table_b, table_c):
        table[208:256, :] = tail
    for b in range(EY):
        wyb = wy[b : b + 1]
        dyb = dy[b : b + 1]
        rows = pl.ds(b * EX, 24)
        table_a[rows, :] = wx * (live_charge * wyb)
        table_b[rows, :] = dx * (along_x * wyb) + wx * (along_y * dyb + direct * wyb)
        table_c[rows, :] = wx * (along_z * wyb)
    nt = ((1,), (1,))
    first = product(zw, split(table_a[...]), nt)
    second = product(zw, split(table_b[...]), nt) + product(zd, split(table_c[...]), nt)
    for field, value in enumerate((first, second)):
        for half in range(2):
            send[pl.ds(field * 2 * K + half, K, stride=2), :] = value[
                :, half * LANES : (half + 1) * LANES
            ]
    spectral[0] = zw[0]
    spectral[1] = zw[1]
    spectral[2] = zd[0]
    spectral[3] = zd[1]
    atoms[0:24, :] = wx
    atoms[24:48, :] = dx
    atoms[48:64, :] = wy
    atoms[64:80, :] = dy
    for row, value in enumerate((live, live_charge, force_cot[0, 0], force_cot[1, 0], force_cot[2, 0])):
        atoms[80 + row : 81 + row, :] = value
    for copy in copies[7:]:
        copy.wait()


def plane_kernel(
    received, hx, hyt, hy, hxt, row_terms, column_terms, send, plane, edges, blocks
):
    device = lax.axis_index("gx") * N_GY + lax.axis_index("gy")
    freq_z = lax.rem(device, K)
    here = lax.broadcasted_iota(jnp.int32, (1, K), 1) == freq_z
    factor_z = jnp.sum(jnp.where(here, row_terms[0:1, :], 0.0), axis=1, keepdims=True)
    square_z = jnp.sum(jnp.where(here, row_terms[1:2, :], 0.0), axis=1, keepdims=True)

    def block(ref_main, ref_edge, b):
        if 1 <= b <= CY:
            return ref_main, (b - 1) * N_GY
        return ref_edge, (0 if b == 0 else b - CY) * N_GY

    plane[:, 256:PAD] = jnp.zeros((K, PAD - 256), jnp.float32)
    edges[:, 256:PAD] = jnp.zeros((3 * N_GY, PAD - 256), jnp.float32)
    for gx in range(N_GX):
        rows = jnp.concatenate(
            [received[pl.ds(gx * 2 * N_GY + half, N_GY, stride=2), :] for half in range(2)], axis=1
        )
        for b in range(EY):
            ref, start = block(plane, edges, b)
            ref[start : start + N_GY, gx * EX : (gx + 1) * EX] = rows[:, b * EX : (b + 1) * EX]
    for edge, m, shift in ((0, 7, N_GY - 1), (1, 0, 1), (2, 1, 1)):
        plane[m * N_GY : (m + 1) * N_GY, :] += pltpu.roll(
            edges[edge * N_GY : (edge + 1) * N_GY, :], shift, 0
        )
    half_way = product(split(plane[...]), (hx[0], hx[1]))
    spectrum = product((hyt[0], hyt[1]), split(half_way))
    total_sq = (column_terms[:, 1:2] + row_terms[1:2, :]) + square_z
    factor = column_terms[:, 0:1] * (row_terms[0:1, :] * (factor_z * (1.0 / (math.pi * K))))
    kernel = jnp.where(total_sq > 0.0, factor / jnp.maximum(total_sq, 1.0), 0.0)
    half_way = product((hy[0], hy[1]), split(spectrum * kernel))
    plane[...] = product(split(half_way), (hxt[0], hxt[1]))
    for edge, m, shift in ((0, 7, 1), (1, 0, N_GY - 1), (2, 1, N_GY - 1)):
        edges[edge * N_GY : (edge + 1) * N_GY, :] = pltpu.roll(
            plane[m * N_GY : (m + 1) * N_GY, :], shift, 0
        )
    blocks[:, LANES:] = jnp.zeros((DEVICES, LANES), jnp.float32)
    for b in range(EY):
        ref, start = block(plane, edges, b)
        rows = ref[start : start + N_GY, :]
        for gx in range(N_GX):
            blocks[gx * N_GY : (gx + 1) * N_GY, b * EX : (b + 1) * EX] = rows[
                :, gx * EX : (gx + 1) * EX
            ]
    for half in range(2):
        send[pl.ds(half, DEVICES, stride=2), :] = blocks[:, half * LANES : (half + 1) * LANES]


def sample_kernel(
    received, spectral, atoms, forces, potential, charge_grad, sample_a, sample_b, sample_c
):
    def field(index):
        halves = [received[pl.ds(index * 2 * K + half, K, stride=2), :] for half in range(2)]
        return split(jnp.concatenate(halves, axis=1).T)

    zw = (spectral[0], spectral[1])
    zd = (spectral[2], spectral[3])
    first = field(0)
    sample_a[...] = product(first, zw)
    sample_b[...] = product(first, zd)
    sample_c[...] = product(field(1), zw)
    wx, dx, wy, dy = atoms[0:24, :], atoms[24:48, :], atoms[48:64, :], atoms[64:80, :]
    live, live_charge, along_x, along_y, along_z = [atoms[80 + row : 81 + row, :] for row in range(5)]
    sums = [jnp.zeros((24, ATOMS), jnp.float32) for _ in range(5)]
    for b in range(EY):
        wyb = wy[b : b + 1]
        dyb = dy[b : b + 1]
        rows = pl.ds(b * EX, 24)
        plain = sample_a[rows, :]
        plain_x = wx * plain
        sums[0] = sums[0] + plain_x * wyb
        sums[1] = sums[1] + (dx * plain) * wyb
        sums[2] = sums[2] + plain_x * dyb
        sums[3] = sums[3] + (wx * sample_b[rows, :]) * wyb
        sums[4] = sums[4] + (wx * sample_c[rows, :]) * wyb
    mesh_value, grad_x, grad_y, grad_z, response = [
        jnp.sum(value, axis=0, keepdims=True) for value in sums
    ]
    forces[0, 0] = -live_charge * grad_x
    forces[1, 0] = -live_charge * grad_y
    forces[2, 0] = -live_charge * grad_z
    potential[0] = live * mesh_value
    charge_grad[0] = live * (response - along_x * grad_x - along_y * grad_y - along_z * grad_z)


def exchange(blocks):
    swapped = lax.all_to_all(
        blocks.reshape(DEVICES, 2, LANES), ("gx", "gy"), split_axis=0, concat_axis=0, tiled=True
    )
    return swapped.reshape(2 * DEVICES, LANES)


def on_device(charge, fraction, base_cell, live_slot, force_cot, potential_cot):
    x, y = plane_coordinates()
    freq = np.arange(K)
    terms = np.stack(influence_factors())
    hx = np.pad(cas_table(x, freq), ((0, PAD - x.size), (0, 0)))
    hy = cas_table(y, freq)
    constants = [split_table(value) for value in (hx, hy.T, hy, hx.T)] + [terms, terms.T]
    params = pltpu.CompilerParams(vmem_limit_bytes=48 * 1024 * 1024)
    vmem = pl.BlockSpec(memory_space=pltpu.VMEM)
    hbm = pl.BlockSpec(memory_space=pltpu.HBM)
    f32 = jnp.float32
    table = pltpu.VMEM((K, ATOMS), f32)
    message = jax.ShapeDtypeStruct((2 * DEVICES, LANES), f32)
    arguments = (charge, fraction, base_cell, live_slot, force_cot, potential_cot)
    hartley = split_table(cas_table(freq, freq))

    sent, spectral, atoms, *tables = pl.pallas_call(
        spread_kernel,
        out_shape=(
            message,
            jax.ShapeDtypeStruct((4, K, ATOMS), jnp.bfloat16),
            jax.ShapeDtypeStruct((88, ATOMS), f32),
            *[jax.ShapeDtypeStruct(value.shape, value.dtype) for value in constants],
        ),
        in_specs=[hbm] * 13,
        out_specs=(vmem,) * 9,
        scratch_shapes=[pltpu.VMEM(value.shape, value.dtype) for value in arguments]
        + [pltpu.VMEM(hartley.shape, hartley.dtype), table, table, table]
        + [pltpu.SemaphoreType.DMA((13,))],
        compiler_params=params,
        name="spread",
    )(*arguments, jnp.asarray(hartley), *[jnp.asarray(value) for value in constants])
    received = exchange(sent)
    solved = pl.pallas_call(
        plane_kernel,
        out_shape=message,
        in_specs=[vmem] * 7,
        out_specs=vmem,
        scratch_shapes=[
            pltpu.VMEM((K, PAD), f32),
            pltpu.VMEM((3 * N_GY, PAD), f32),
            pltpu.VMEM((DEVICES, 2 * LANES), f32),
        ],
        compiler_params=params,
        name="plane",
    )(received, *tables)
    returned = exchange(solved)
    return pl.pallas_call(
        sample_kernel,
        out_shape=(
            jax.ShapeDtypeStruct((3, 1, 1, ATOMS), f32),
            jax.ShapeDtypeStruct((1, 1, ATOMS), f32),
            jax.ShapeDtypeStruct((1, 1, ATOMS), f32),
        ),
        in_specs=[vmem] * 3,
        out_specs=(vmem, vmem, vmem),
        scratch_shapes=[table, table, table],
        compiler_params=params,
        name="sample",
    )(returned, spectral, atoms)


def solution(mesh):
    return jax.shard_map(
        on_device,
        mesh=mesh,
        in_specs=(
            P("gx", "gy", None),
            P(None, "gx", "gy", None),
            P("gx", "gy", None),
            P("gx", "gy", None),
            P(None, "gx", "gy", None),
            P("gx", "gy", None),
        ),
        out_specs=(P(None, "gx", "gy", None), P("gx", "gy", None), P("gx", "gy", None)),
        check_vma=False,
    )
```

```python
import math

import jax
import jax.numpy as jnp
import ml_dtypes
import numpy as np
from jax import lax
from jax.experimental import pallas as pl
from jax.experimental.pallas import tpu as pltpu
from jax.sharding import PartitionSpec as P

K = 256
CX = 16
CY = 8
EX = CX + 3
EY = CY + 3
N_GX = 16
N_GY = 32
ATOMS = 256
DEVICES = N_GX * N_GY
LANES = 128
PAD = 384
SPREAD_GRANT = 60 * 1024 * 1024

EWALD_SPLIT = 0.8


def cas_table(left, right):
    angles = 2.0 * math.pi / K * (left[:, None] * right[None, :] % K)
    return np.cos(angles) + np.sin(angles)


def split_table(table):
    high = table.astype(np.float32).astype(ml_dtypes.bfloat16)
    low = (table - high.astype(np.float64)).astype(np.float32).astype(ml_dtypes.bfloat16)
    return np.stack([high, low])


def plane_coordinates():
    gx, a = np.meshgrid(np.arange(N_GX), np.arange(EX), indexing="ij")
    ext_x = (gx * CX + a - 1).reshape(-1) % K
    m, gy = np.meshgrid(np.arange(CY), np.arange(N_GY), indexing="ij")
    return ext_x, (gy * CY + m).reshape(-1)


def natural(index):
    return jnp.bitwise_or(
        jnp.left_shift(jnp.bitwise_and(index, N_GY - 1), 3), jnp.right_shift(index, 5)
    )


def influence_factors():
    freq = np.arange(K)
    nearest = np.minimum(freq, K - freq).astype(np.float64)
    damping = math.pi * math.pi / (EWALD_SPLIT * EWALD_SPLIT * K * K)
    cosine = np.cos(2.0 * math.pi / K * freq)
    factor = np.exp(-damping * nearest * nearest) * 9.0 / (2.0 + cosine) ** 2
    return factor.astype(np.float32), (nearest * nearest).astype(np.float32)


def split(value):
    high = value.astype(jnp.bfloat16)
    low = (value - high.astype(jnp.float32)).astype(jnp.bfloat16)
    return high, low


def product(left, right, dims=((1,), (0,))):
    def one(a, b):
        return lax.dot_general(a, b, (dims, ((), ())), preferred_element_type=jnp.float32)

    return one(left[0], right[0]) + (one(left[0], right[1]) + one(left[1], right[0]))


def spline_terms(fraction):
    square = fraction * fraction
    cubic_part = square * fraction
    remain = 1.0 - fraction
    weights = (
        remain * remain * remain * (1.0 / 6.0),
        (3.0 * cubic_part - 6.0 * square + 4.0) * (1.0 / 6.0),
        (-3.0 * cubic_part + 3.0 * square + 3.0 * fraction + 1.0) * (1.0 / 6.0),
        cubic_part * (1.0 / 6.0),
    )
    slopes = (
        -0.5 * remain * remain,
        (3.0 * square - 4.0 * fraction) * 0.5,
        (-3.0 * square + 2.0 * fraction + 1.0) * 0.5,
        0.5 * square,
    )
    return weights, slopes


def banded(place, terms):
    hits = [place == offset for offset in range(4)]

    def table(values):
        out = jnp.zeros(place.shape, jnp.float32)
        for hit, value in zip(hits, values):
            out = jnp.where(hit, jnp.broadcast_to(value, place.shape), out)
        return out

    return [table(values) for values in terms]


def row_numbers(rows):
    return lax.broadcasted_iota(jnp.int32, (rows, ATOMS), 0)


def domain_tables(cells, fraction_ref):
    cell_x = jnp.right_shift(cells, 7)
    cell_y = jnp.bitwise_and(jnp.right_shift(cells, 4), CY - 1)
    wx, dx = banded(row_numbers(24) - cell_x, spline_terms(fraction_ref[0, 0]))
    wy, dy = banded(row_numbers(16) - cell_y, spline_terms(fraction_ref[1, 0]))
    return wx, dx, wy, dy


def spread_kernel(
    charge_in, fraction_in, cell_in, live_in, force_in, potential_in, hartley_in,
    send_out, spectral_out, atoms_out,
    charge, fraction, base_cell, live_slot, force_cot, potential_cot, hartley,
    table_a, table_b, table_c, send, spectral, atoms, arrived, left,
):
    pairs = (
        (cell_in, base_cell),
        (fraction_in, fraction),
        (hartley_in, hartley),
        (charge_in, charge),
        (live_in, live_slot),
        (force_in, force_cot),
        (potential_in, potential_cot),
    )
    copies = [
        pltpu.make_async_copy(source, target, arrived.at[index])
        for index, (source, target) in enumerate(pairs)
    ]
    for copy in copies:
        copy.start()
    half = slice(0, 2 * K), slice(2 * K, 4 * K)
    results = [
        pltpu.make_async_copy(source, target, left.at[index])
        for index, (source, target) in enumerate((
            (send.at[half[0]], send_out.at[half[0]]),
            (send.at[half[1]], send_out.at[half[1]]),
            (spectral, spectral_out),
            (atoms, atoms_out),
        ))
    ]

    def store(field, value):
        for part in range(2):
            send[pl.ds(field * 2 * K + part, K, stride=2), :] = value[
                :, part * LANES : (part + 1) * LANES
            ]
        results[field].start()

    for copy in copies[0:2]:
        copy.wait()
    cells = base_cell[0]
    slot = lax.broadcasted_iota(jnp.int32, (1, ATOMS), 1)
    base_z = jnp.bitwise_and(slot, -16) + jnp.bitwise_and(cells, 15)
    place_z = jnp.bitwise_and(natural(row_numbers(K)) - (base_z - 1), K - 1)
    wz, dz = banded(place_z, spline_terms(fraction[2, 0]))
    wx, dx, wy, dy = domain_tables(cells, fraction)
    copies[2].wait()
    hart = (hartley[0], hartley[1])
    zw = split(product(hart, split(wz)))
    for copy in copies[3:]:
        copy.wait()
    live = live_slot[0].astype(jnp.float32)
    live_charge = charge[0] * live
    along_x = -live_charge * force_cot[0, 0]
    along_y = -live_charge * force_cot[1, 0]
    along_z = -live_charge * force_cot[2, 0]
    direct = live * potential_cot[0]
    tail = jnp.zeros((48, ATOMS), jnp.float32)
    for table in (table_a, table_b, table_c):
        table[208:256, :] = tail
    for b in range(EY):
        wyb = wy[b : b + 1]
        dyb = dy[b : b + 1]
        rows = pl.ds(b * EX, 24)
        table_a[rows, :] = wx * (live_charge * wyb)
        table_b[rows, :] = dx * (along_x * wyb) + wx * (along_y * dyb + direct * wyb)
        table_c[rows, :] = wx * (along_z * wyb)
    nt = ((1,), (1,))
    store(0, product(zw, split(table_a[...]), nt))
    zd = split(product(hart, split(dz)))
    store(1, product(zw, split(table_b[...]), nt) + product(zd, split(table_c[...]), nt))
    spectral[0] = zw[0]
    spectral[1] = zw[1]
    spectral[2] = zd[0]
    spectral[3] = zd[1]
    results[2].start()
    atoms[0:24, :] = wx
    atoms[24:48, :] = dx
    atoms[48:64, :] = wy
    atoms[64:80, :] = dy
    scalars = (live, live_charge, force_cot[0, 0], force_cot[1, 0], force_cot[2, 0])
    for row, value in enumerate(scalars):
        atoms[80 + row : 81 + row, :] = value
    atoms[85:88, :] = jnp.zeros((3, ATOMS), jnp.float32)
    results[3].start()
    for copy in results:
        copy.wait()


def plane_kernel(
    received, hartley, tables, send, plane, edges, blocks
):
    device = lax.axis_index("gx") * N_GY + lax.axis_index("gy")
    here = lax.broadcasted_iota(jnp.int32, (1, K), 1) == lax.rem(device, K)
    factor_x, square_x, factor_y, square_y = [tables[PAD + row : PAD + row + 1, :] for row in range(4)]
    factor_z = jnp.sum(jnp.where(here, factor_y, 0.0), axis=1, keepdims=True)
    square_z = jnp.sum(jnp.where(here, square_y, 0.0), axis=1, keepdims=True)
    hy = (hartley[0], hartley[1])
    hx = split(tables[0:PAD, :])

    def block(ref_main, ref_edge, b):
        if 1 <= b <= CY:
            return ref_main, (b - 1) * N_GY
        return ref_edge, (0 if b == 0 else b - CY) * N_GY

    plane[:, 256:PAD] = jnp.zeros((K, PAD - 256), jnp.float32)
    edges[:, 256:PAD] = jnp.zeros((3 * N_GY, PAD - 256), jnp.float32)
    for gx in range(N_GX):
        rows = jnp.concatenate(
            [received[pl.ds(gx * 2 * N_GY + half, N_GY, stride=2), :] for half in range(2)], axis=1
        )
        for b in range(EY):
            ref, start = block(plane, edges, b)
            ref[start : start + N_GY, gx * EX : (gx + 1) * EX] = rows[:, b * EX : (b + 1) * EX]
    for edge, m, shift in ((0, 7, N_GY - 1), (1, 0, 1), (2, 1, 1)):
        plane[m * N_GY : (m + 1) * N_GY, :] += pltpu.roll(
            edges[edge * N_GY : (edge + 1) * N_GY, :], shift, 0
        )
    half_way = product(split(plane[...]), hx)
    spectrum = product(hy, split(half_way))
    total_sq = jnp.transpose(square_y) + (square_x + square_z)
    factor = jnp.transpose(factor_y) * (factor_x * (factor_z * (1.0 / (math.pi * K))))
    kernel = jnp.where(total_sq > 0.0, factor / jnp.maximum(total_sq, 1.0), 0.0)
    half_way = product(hy, split(spectrum * kernel))
    plane[...] = product(split(half_way), hx, ((1,), (1,)))
    for edge, m, shift in ((0, 7, 1), (1, 0, N_GY - 1), (2, 1, N_GY - 1)):
        edges[edge * N_GY : (edge + 1) * N_GY, :] = pltpu.roll(
            plane[m * N_GY : (m + 1) * N_GY, :], shift, 0
        )
    blocks[:, LANES:] = jnp.zeros((DEVICES, LANES), jnp.float32)
    for b in range(EY):
        ref, start = block(plane, edges, b)
        rows = ref[start : start + N_GY, :]
        for gx in range(N_GX):
            blocks[gx * N_GY : (gx + 1) * N_GY, b * EX : (b + 1) * EX] = rows[
                :, gx * EX : (gx + 1) * EX
            ]
    for half in range(2):
        send[pl.ds(half, DEVICES, stride=2), :] = blocks[:, half * LANES : (half + 1) * LANES]


def sample_kernel(
    received, spectral, atoms, forces, potential, charge_grad, sample_a, sample_b, sample_c
):
    def field(index):
        halves = [received[pl.ds(index * 2 * K + half, K, stride=2), :] for half in range(2)]
        return split(jnp.concatenate(halves, axis=1).T)

    zw = (spectral[0], spectral[1])
    zd = (spectral[2], spectral[3])
    first = field(0)
    sample_a[...] = product(first, zw)
    sample_b[...] = product(first, zd)
    sample_c[...] = product(field(1), zw)
    wx, dx, wy, dy = atoms[0:24, :], atoms[24:48, :], atoms[48:64, :], atoms[64:80, :]
    live, live_charge, along_x, along_y, along_z = [atoms[80 + row : 81 + row, :] for row in range(5)]
    sums = [jnp.zeros((24, ATOMS), jnp.float32) for _ in range(5)]
    for b in range(EY):
        wyb = wy[b : b + 1]
        dyb = dy[b : b + 1]
        rows = pl.ds(b * EX, 24)
        plain = sample_a[rows, :]
        plain_x = wx * plain
        sums[0] = sums[0] + plain_x * wyb
        sums[1] = sums[1] + (dx * plain) * wyb
        sums[2] = sums[2] + plain_x * dyb
        sums[3] = sums[3] + (wx * sample_b[rows, :]) * wyb
        sums[4] = sums[4] + (wx * sample_c[rows, :]) * wyb
    mesh_value, grad_x, grad_y, grad_z, response = [
        jnp.sum(value, axis=0, keepdims=True) for value in sums
    ]
    forces[0, 0] = -live_charge * grad_x
    forces[1, 0] = -live_charge * grad_y
    forces[2, 0] = -live_charge * grad_z
    potential[0] = live * mesh_value
    charge_grad[0] = live * (response - along_x * grad_x - along_y * grad_y - along_z * grad_z)


def exchange(blocks):
    swapped = lax.all_to_all(
        blocks.reshape(DEVICES, 2, LANES), ("gx", "gy"), split_axis=0, concat_axis=0, tiled=True
    )
    return swapped.reshape(2 * DEVICES, LANES)


def on_device(charge, fraction, base_cell, live_slot, force_cot, potential_cot):
    x, y = plane_coordinates()
    freq = np.arange(K)
    hartley = split_table(cas_table(y, y))
    factor, square = influence_factors()
    tables = np.zeros((PAD + 8, K), np.float32)
    tables[: x.size] = cas_table(x, freq)
    tables[PAD : PAD + 4] = factor, square, factor[y], square[y]
    params = pltpu.CompilerParams(vmem_limit_bytes=48 * 1024 * 1024)
    vmem = pl.BlockSpec(memory_space=pltpu.VMEM)
    hbm = pl.BlockSpec(memory_space=pltpu.HBM)
    f32 = jnp.float32
    table = pltpu.VMEM((K, ATOMS), f32)
    message = jax.ShapeDtypeStruct((2 * DEVICES, LANES), f32)
    arguments = (charge, fraction, base_cell, live_slot, force_cot, potential_cot)

    sent, spectral, atoms = pl.pallas_call(
        spread_kernel,
        out_shape=(
            message,
            jax.ShapeDtypeStruct((4, K, ATOMS), jnp.bfloat16),
            jax.ShapeDtypeStruct((88, ATOMS), f32),
        ),
        in_specs=[hbm] * 7,
        out_specs=(hbm,) * 3,
        scratch_shapes=[pltpu.VMEM(value.shape, value.dtype) for value in arguments]
        + [pltpu.VMEM(hartley.shape, hartley.dtype), table, table, table]
        + [pltpu.VMEM((2 * DEVICES, LANES), f32), pltpu.VMEM((4, K, ATOMS), jnp.bfloat16)]
        + [pltpu.VMEM((88, ATOMS), f32), pltpu.SemaphoreType.DMA((7,)), pltpu.SemaphoreType.DMA((4,))],
        compiler_params=pltpu.CompilerParams(vmem_limit_bytes=SPREAD_GRANT),
        name="spread",
    )(*arguments, jnp.asarray(hartley))
    received = exchange(sent)
    solved = pl.pallas_call(
        plane_kernel,
        out_shape=message,
        in_specs=[vmem] * 3,
        out_specs=vmem,
        scratch_shapes=[
            pltpu.VMEM((K, PAD), f32),
            pltpu.VMEM((3 * N_GY, PAD), f32),
            pltpu.VMEM((DEVICES, 2 * LANES), f32),
        ],
        compiler_params=params,
        name="plane",
    )(received, jnp.asarray(hartley), jnp.asarray(tables))
    returned = exchange(solved)
    return pl.pallas_call(
        sample_kernel,
        out_shape=(
            jax.ShapeDtypeStruct((3, 1, 1, ATOMS), f32),
            jax.ShapeDtypeStruct((1, 1, ATOMS), f32),
            jax.ShapeDtypeStruct((1, 1, ATOMS), f32),
        ),
        in_specs=[vmem] * 3,
        out_specs=(vmem, vmem, vmem),
        scratch_shapes=[table, table, table],
        compiler_params=params,
        name="sample",
    )(returned, spectral, atoms)


def solution(mesh):
    return jax.shard_map(
        on_device,
        mesh=mesh,
        in_specs=(
            P("gx", "gy", None),
            P(None, "gx", "gy", None),
            P("gx", "gy", None),
            P("gx", "gy", None),
            P(None, "gx", "gy", None),
            P("gx", "gy", None),
        ),
        out_specs=(P(None, "gx", "gy", None), P("gx", "gy", None), P("gx", "gy", None)),
        check_vma=False,
    )
```

```python
import math

import jax
import jax.numpy as jnp
import ml_dtypes
import numpy as np
from jax import lax
from jax.experimental import pallas as pl
from jax.experimental.pallas import tpu as pltpu
from jax.sharding import PartitionSpec as P

K = 256
CY = 8
N_GX = 16
N_GY = 32
ATOMS = 256
DEVICES = N_GX * N_GY
LANES = 128
SCALARS = 256
SPREAD_GRANT = 60 * 1024 * 1024

EWALD_SPLIT = 0.8


def cas_table(left, right):
    angles = 2.0 * math.pi / K * (left[:, None] * right[None, :] % K)
    return np.cos(angles) + np.sin(angles)


def split_table(table):
    high = table.astype(np.float32).astype(ml_dtypes.bfloat16)
    low = (table - high.astype(np.float64)).astype(np.float32).astype(ml_dtypes.bfloat16)
    return np.stack([high, low])


def plane_rows():
    m, gy = np.meshgrid(np.arange(CY), np.arange(N_GY), indexing="ij")
    return (gy * CY + m).reshape(-1)


def natural(index):
    return jnp.bitwise_or(
        jnp.left_shift(jnp.bitwise_and(index, N_GY - 1), 3), jnp.right_shift(index, 5)
    )


def influence_factors():
    freq = np.arange(K)
    nearest = np.minimum(freq, K - freq).astype(np.float64)
    damping = math.pi * math.pi / (EWALD_SPLIT * EWALD_SPLIT * K * K)
    cosine = np.cos(2.0 * math.pi / K * freq)
    factor = np.exp(-damping * nearest * nearest) * 9.0 / (2.0 + cosine) ** 2
    return factor.astype(np.float32), (nearest * nearest).astype(np.float32)


def split(value):
    high = value.astype(jnp.bfloat16)
    low = (value - high.astype(jnp.float32)).astype(jnp.bfloat16)
    return high, low


def product(left, right, dims=((1,), (0,))):
    def one(a, b):
        return lax.dot_general(a, b, (dims, ((), ())), preferred_element_type=jnp.float32)

    return one(left[0], right[0]) + (one(left[0], right[1]) + one(left[1], right[0]))


def spline_terms(fraction):
    square = fraction * fraction
    cubic_part = square * fraction
    remain = 1.0 - fraction
    weights = (
        remain * remain * remain * (1.0 / 6.0),
        (3.0 * cubic_part - 6.0 * square + 4.0) * (1.0 / 6.0),
        (-3.0 * cubic_part + 3.0 * square + 3.0 * fraction + 1.0) * (1.0 / 6.0),
        cubic_part * (1.0 / 6.0),
    )
    slopes = (
        -0.5 * remain * remain,
        (3.0 * square - 4.0 * fraction) * 0.5,
        (-3.0 * square + 2.0 * fraction + 1.0) * 0.5,
        0.5 * square,
    )
    return weights, slopes


def banded(place, terms):
    hits = [place == offset for offset in range(4)]

    def table(values):
        out = jnp.zeros(place.shape, jnp.float32)
        for hit, value in zip(hits, values):
            out = jnp.where(hit, jnp.broadcast_to(value, place.shape), out)
        return out

    return [table(values) for values in terms]


def row_numbers(rows):
    return lax.broadcasted_iota(jnp.int32, (rows, ATOMS), 0)


SHIFT_X = 53
SHIFT_XY = 57
EDGES = {0: 8, 1: 9, 7: -1}


def halo_x(lane):
    low = (lane == 15) | (lane == 4) | (lane == 8)
    upper = (lane == 0) | (lane == 5) | (lane == 9)
    top = (lane == 1) | (lane == 6) | (lane == 10)
    return jnp.where(low, -1, jnp.where(upper, 16, jnp.where(top, 17, 99)))


def halo_y(lane, j):
    before, behind = (j - 4) % 8, (j - 3) % 8
    choice = (
        ((lane <= 1) | (lane == 15), j),
        (lane == 4, before if before in EDGES else 99),
        ((lane == 5) | (lane == 6), behind if behind in EDGES else 99),
        (lane == 8, EDGES.get(before, 99)),
        ((lane == 9) | (lane == 10), EDGES.get(behind, 99)),
    )
    out = jnp.full(lane.shape, 99, jnp.int32)
    for mask, y in choice:
        out = jnp.where(mask, y, out)
    return out


def domain_tables(cells, fraction_ref):
    cell_x = jnp.right_shift(cells, 7) - 1
    cell_y = jnp.bitwise_and(jnp.right_shift(cells, 4), CY - 1) - 1
    terms_x = spline_terms(fraction_ref[0, 0])
    terms_y = spline_terms(fraction_ref[1, 0])
    lane = row_numbers(16)
    out = banded(lane - cell_x, terms_x) + banded(halo_x(lane) - cell_x, terms_x)
    out += banded(lane - 1 - cell_y, terms_y)
    for j in range(2, 7):
        out += banded(halo_y(lane, j) - cell_y, terms_y)
    return out


def message_blocks(tables):
    wx, dx, wx_halo, dx_halo, wy, dy = tables[:6]

    def row(y):
        return wy[y + 1 : y + 2], dy[y + 1 : y + 2]

    blocks = [(wx, dx) + row(m) for m in range(CY)]
    for j in range(8):
        if j in EDGES:
            blocks.append((wx, dx) + row(EDGES[j]))
        else:
            blocks.append((wx_halo, dx_halo, tables[2 + 2 * j], tables[3 + 2 * j]))
    return blocks


def spread_kernel(
    charge_in, fraction_in, cell_in, live_in, force_in, potential_in, hartley_in,
    send_out, spectral_out, atoms_out,
    charge, fraction, base_cell, live_slot, force_cot, potential_cot, hartley,
    table_a, table_b, table_c, send, spectral, atoms, arrived, left,
):
    pairs = (
        (cell_in, base_cell),
        (fraction_in, fraction),
        (hartley_in, hartley),
        (charge_in, charge),
        (live_in, live_slot),
        (force_in, force_cot),
        (potential_in, potential_cot),
    )
    copies = [
        pltpu.make_async_copy(source, target, arrived.at[index])
        for index, (source, target) in enumerate(pairs)
    ]
    for copy in copies:
        copy.start()
    half = slice(0, 2 * K), slice(2 * K, 4 * K)
    part = slice(0, 2), slice(2, 4)
    results = [
        pltpu.make_async_copy(source, target, left.at[index])
        for index, (source, target) in enumerate((
            (send.at[half[0]], send_out.at[half[0]]),
            (send.at[half[1]], send_out.at[half[1]]),
            (spectral.at[part[0]], spectral_out.at[part[0]]),
            (spectral.at[part[1]], spectral_out.at[part[1]]),
            (atoms, atoms_out),
        ))
    ]

    def store(field, value):
        for row in range(2):
            send[pl.ds(field * 2 * K + row, K, stride=2), :] = value[
                :, row * LANES : (row + 1) * LANES
            ]
        results[field].start()

    def transformed(first, table):
        value = split(product(hart, split(table)))
        spectral[first] = value[0]
        spectral[first + 1] = value[1]
        results[2 + first // 2].start()
        return value

    for copy in copies[0:2]:
        copy.wait()
    cells = base_cell[0]
    slot = lax.broadcasted_iota(jnp.int32, (1, ATOMS), 1)
    base_z = jnp.bitwise_and(slot, -16) + jnp.bitwise_and(cells, 15)
    place_z = jnp.bitwise_and(natural(row_numbers(K)) - (base_z - 1), K - 1)
    wz, dz = banded(place_z, spline_terms(fraction[2, 0]))
    tables = domain_tables(cells, fraction)
    for index, value in enumerate(tables):
        atoms[index * 16 : (index + 1) * 16, :] = value
    for copy in copies[3:]:
        copy.wait()
    live = live_slot[0].astype(jnp.float32)
    live_charge = charge[0] * live
    scalars = (live, live_charge, force_cot[0, 0], force_cot[1, 0], force_cot[2, 0])
    for row, value in enumerate(scalars):
        atoms[SCALARS + row : SCALARS + row + 1, :] = value
    atoms[SCALARS + 5 : SCALARS + 8, :] = jnp.zeros((3, ATOMS), jnp.float32)
    results[4].start()
    along_x = -live_charge * force_cot[0, 0]
    along_y = -live_charge * force_cot[1, 0]
    along_z = -live_charge * force_cot[2, 0]
    direct = live * potential_cot[0]
    for index, (wx, dx, wy, dy) in enumerate(message_blocks(tables)):
        rows = slice(index * 16, (index + 1) * 16)
        table_a[rows, :] = wx * (live_charge * wy)
        table_b[rows, :] = dx * (along_x * wy) + wx * (along_y * dy + direct * wy)
        table_c[rows, :] = wx * (along_z * wy)
    copies[2].wait()
    hart = (hartley[0], hartley[1])
    nt = ((1,), (1,))
    zw = transformed(0, wz)
    store(0, product(zw, split(table_a[...]), nt))
    zd = transformed(2, dz)
    store(1, product(zw, split(table_b[...]), nt) + product(zd, split(table_c[...]), nt))
    for copy in results:
        copy.wait()


def transposed_blocks(values):
    values = list(values)
    block = jnp.right_shift(lax.broadcasted_iota(jnp.int32, values[0].shape, 1), 4)
    for step in (1, 2, 4):
        upper = jnp.bitwise_and(block, step) != 0
        for i in range(8):
            if i & step == 0:
                first, second = values[i], values[i + step]
                values[i] = jnp.where(upper, pltpu.roll(second, 16 * step, 1), first)
                values[i + step] = jnp.where(upper, second, pltpu.roll(first, LANES - 16 * step, 1))
    return values


def plane_kernel(received, hartley, hartley_x, terms, send, plane):
    device = lax.axis_index("gx") * N_GY + lax.axis_index("gy")
    here = lax.broadcasted_iota(jnp.int32, (1, K), 1) == lax.rem(device, K)
    factor_x, square_x, factor_y, square_y = [terms[row : row + 1, :] for row in range(4)]
    factor_z = jnp.sum(jnp.where(here, factor_y, 0.0), axis=1, keepdims=True)
    square_z = jnp.sum(jnp.where(here, square_y, 0.0), axis=1, keepdims=True)
    hy = (hartley[0], hartley[1])
    hx = (hartley_x[0], hartley_x[1])
    place = lax.broadcasted_iota(jnp.int32, (N_GY, LANES), 1)
    block = jnp.right_shift(place, 4)
    lane = jnp.bitwise_and(place, 15)
    low = lane == 15
    high = lane <= 1
    last = block == 7
    first = block <= 1
    edge = last | first

    def rows(gx, half):
        return pl.ds(gx * 2 * N_GY + half, N_GY, stride=2)

    along_x, corners = [], []
    for gx in range(N_GX):
        halo = received[rows(gx, 1), :]
        along_x.append(jnp.where(edge, pltpu.roll(halo, LANES - SHIFT_X, 1), halo))
        corners.append(pltpu.roll(halo, LANES - SHIFT_XY, 1))

    def from_sides(values, gx):
        after, before = values[(gx + 1) % N_GX], values[gx - 1]
        return jnp.where(low, after, jnp.where(high, before, 0.0))

    folded = []
    for gx in range(N_GX):
        own = received[rows(gx, 0), :] + from_sides(along_x, gx)
        side = received[rows(gx, 1), :] + from_sides(corners, gx)
        after, before = pltpu.roll(side, N_GY - 1, 0), pltpu.roll(side, 1, 0)
        folded.append(own + jnp.where(last, after, jnp.where(first, before, 0.0)))
    for group in range(2):
        lines = transposed_blocks(folded[group * 8 : group * 8 + 8])
        for m, line in enumerate(lines):
            plane[m * N_GY : (m + 1) * N_GY, group * LANES : (group + 1) * LANES] = line
    half_way = product(split(plane[...]), hx)
    spectrum = product(hy, split(half_way))
    total_sq = jnp.transpose(square_y) + (square_x + square_z)
    factor = jnp.transpose(factor_y) * (factor_x * (factor_z * (1.0 / (math.pi * K))))
    kernel = jnp.where(total_sq > 0.0, factor / jnp.maximum(total_sq, 1.0), 0.0)
    half_way = product(hy, split(spectrum * kernel))
    plane[...] = product(split(half_way), hx)
    own = []
    for group in range(2):
        own += transposed_blocks(
            plane[m * N_GY : (m + 1) * N_GY, group * LANES : (group + 1) * LANES] for m in range(CY)
        )
    sides = [
        jnp.where(last, pltpu.roll(value, 1, 0), pltpu.roll(value, N_GY - 1, 0)) for value in own
    ]

    def to_sides(values, gx):
        return jnp.where(low, values[gx - 1], values[(gx + 1) % N_GX])

    turned_x = (lane >= 4) & (lane <= 6)
    turned_xy = (lane >= 8) & (lane <= 10)
    for gx in range(N_GX):
        cells_x = to_sides(own, gx)
        cells_xy = to_sides(sides, gx)
        halo = jnp.where(turned_x, pltpu.roll(cells_x, SHIFT_X, 1), cells_x)
        halo = jnp.where(turned_xy, pltpu.roll(cells_xy, SHIFT_XY, 1), halo)
        send[rows(gx, 0), :] = own[gx]
        send[rows(gx, 1), :] = jnp.where(edge, sides[gx], halo)


def sample_kernel(
    received, spectral, atoms, forces, potential, charge_grad, sample_a, sample_b, sample_c
):
    def field(index):
        halves = [received[pl.ds(index * 2 * K + half, K, stride=2), :] for half in range(2)]
        return split(jnp.concatenate(halves, axis=1).T)

    zw = (spectral[0], spectral[1])
    zd = (spectral[2], spectral[3])
    first = field(0)
    sample_a[...] = product(first, zw)
    sample_b[...] = product(first, zd)
    sample_c[...] = product(field(1), zw)
    live, live_charge, along_x, along_y, along_z = [
        atoms[SCALARS + row : SCALARS + row + 1, :] for row in range(5)
    ]
    tables = [atoms[index * 16 : (index + 1) * 16, :] for index in range(16)]
    sums = [jnp.zeros((16, ATOMS), jnp.float32) for _ in range(5)]
    for index, (wx, dx, wy, dy) in enumerate(message_blocks(tables)):
        rows = slice(index * 16, (index + 1) * 16)
        plain = sample_a[rows, :]
        plain_x = wx * plain
        sums[0] = sums[0] + plain_x * wy
        sums[1] = sums[1] + (dx * plain) * wy
        sums[2] = sums[2] + plain_x * dy
        sums[3] = sums[3] + (wx * sample_b[rows, :]) * wy
        sums[4] = sums[4] + (wx * sample_c[rows, :]) * wy
    mesh_value, grad_x, grad_y, grad_z, response = [
        jnp.sum(value, axis=0, keepdims=True) for value in sums
    ]
    forces[0, 0] = -live_charge * grad_x
    forces[1, 0] = -live_charge * grad_y
    forces[2, 0] = -live_charge * grad_z
    potential[0] = live * mesh_value
    charge_grad[0] = live * (response - along_x * grad_x - along_y * grad_y - along_z * grad_z)


def exchange(blocks):
    swapped = lax.all_to_all(
        blocks.reshape(DEVICES, 2, LANES), ("gx", "gy"), split_axis=0, concat_axis=0, tiled=True
    )
    return swapped.reshape(2 * DEVICES, LANES)


def on_device(charge, fraction, base_cell, live_slot, force_cot, potential_cot):
    y = plane_rows()
    freq = np.arange(K)
    hartley = split_table(cas_table(y, y))
    hartley_x = split_table(cas_table(freq, freq))
    factor, square = influence_factors()
    terms = np.zeros((8, K), np.float32)
    terms[:4] = factor, square, factor[y], square[y]
    params = pltpu.CompilerParams(vmem_limit_bytes=48 * 1024 * 1024)
    vmem = pl.BlockSpec(memory_space=pltpu.VMEM)
    hbm = pl.BlockSpec(memory_space=pltpu.HBM)
    f32 = jnp.float32
    table = pltpu.VMEM((K, ATOMS), f32)
    message = jax.ShapeDtypeStruct((2 * DEVICES, LANES), f32)
    arguments = (charge, fraction, base_cell, live_slot, force_cot, potential_cot)

    sent, spectral, atoms = pl.pallas_call(
        spread_kernel,
        out_shape=(
            message,
            jax.ShapeDtypeStruct((4, K, ATOMS), jnp.bfloat16),
            jax.ShapeDtypeStruct((SCALARS + 8, ATOMS), f32),
        ),
        in_specs=[hbm] * 7,
        out_specs=(hbm,) * 3,
        scratch_shapes=[pltpu.VMEM(value.shape, value.dtype) for value in arguments]
        + [pltpu.VMEM(hartley.shape, hartley.dtype), table, table, table]
        + [pltpu.VMEM((2 * DEVICES, LANES), f32), pltpu.VMEM((4, K, ATOMS), jnp.bfloat16)]
        + [pltpu.VMEM((SCALARS + 8, ATOMS), f32), pltpu.SemaphoreType.DMA((7,)), pltpu.SemaphoreType.DMA((5,))],
        compiler_params=pltpu.CompilerParams(vmem_limit_bytes=SPREAD_GRANT),
        name="spread",
    )(*arguments, jnp.asarray(hartley))
    received = exchange(sent)
    solved = pl.pallas_call(
        plane_kernel,
        out_shape=message,
        in_specs=[vmem] * 4,
        out_specs=vmem,
        scratch_shapes=[pltpu.VMEM((K, K), f32)],
        compiler_params=params,
        name="plane",
    )(received, jnp.asarray(hartley), jnp.asarray(hartley_x), jnp.asarray(terms))
    returned = exchange(solved)
    return pl.pallas_call(
        sample_kernel,
        out_shape=(
            jax.ShapeDtypeStruct((3, 1, 1, ATOMS), f32),
            jax.ShapeDtypeStruct((1, 1, ATOMS), f32),
            jax.ShapeDtypeStruct((1, 1, ATOMS), f32),
        ),
        in_specs=[vmem] * 3,
        out_specs=(vmem, vmem, vmem),
        scratch_shapes=[table, table, table],
        compiler_params=params,
        name="sample",
    )(returned, spectral, atoms)


def solution(mesh):
    return jax.shard_map(
        on_device,
        mesh=mesh,
        in_specs=(
            P("gx", "gy", None),
            P(None, "gx", "gy", None),
            P("gx", "gy", None),
            P("gx", "gy", None),
            P(None, "gx", "gy", None),
            P("gx", "gy", None),
        ),
        out_specs=(P(None, "gx", "gy", None), P("gx", "gy", None), P("gx", "gy", None)),
        check_vma=False,
    )
```

```python
import math

import jax
import jax.numpy as jnp
import ml_dtypes
import numpy as np
from jax import lax
from jax.experimental import pallas as pl
from jax.experimental.pallas import tpu as pltpu
from jax.sharding import PartitionSpec as P

K = 256
CY = 8
N_GX = 16
N_GY = 32
ATOMS = 256
DEVICES = N_GX * N_GY
LANES = 128
SCALARS = 256

EWALD_SPLIT = 0.8


def cas_table(left, right):
    angles = 2.0 * math.pi / K * (left[:, None] * right[None, :] % K)
    return np.cos(angles) + np.sin(angles)


def split_table(table):
    high = table.astype(np.float32).astype(ml_dtypes.bfloat16)
    low = (table - high.astype(np.float64)).astype(np.float32).astype(ml_dtypes.bfloat16)
    return np.stack([high, low])


def plane_rows():
    m, gy = np.meshgrid(np.arange(CY), np.arange(N_GY), indexing="ij")
    return (gy * CY + m).reshape(-1)


def natural(index):
    return jnp.bitwise_or(
        jnp.left_shift(jnp.bitwise_and(index, N_GY - 1), 3), jnp.right_shift(index, 5)
    )


def influence_factors():
    freq = np.arange(K)
    nearest = np.minimum(freq, K - freq).astype(np.float64)
    damping = math.pi * math.pi / (EWALD_SPLIT * EWALD_SPLIT * K * K)
    cosine = np.cos(2.0 * math.pi / K * freq)
    factor = np.exp(-damping * nearest * nearest) * 9.0 / (2.0 + cosine) ** 2
    return factor.astype(np.float32), (nearest * nearest).astype(np.float32)


def split(value):
    high = value.astype(jnp.bfloat16)
    low = (value - high.astype(jnp.float32)).astype(jnp.bfloat16)
    return high, low


def product(left, right, dims=((1,), (0,))):
    def one(a, b):
        return lax.dot_general(a, b, (dims, ((), ())), preferred_element_type=jnp.float32)

    return one(left[0], right[0]) + (one(left[0], right[1]) + one(left[1], right[0]))


def spline_terms(fraction):
    square = fraction * fraction
    cubic_part = square * fraction
    remain = 1.0 - fraction
    weights = (
        remain * remain * remain * (1.0 / 6.0),
        (3.0 * cubic_part - 6.0 * square + 4.0) * (1.0 / 6.0),
        (-3.0 * cubic_part + 3.0 * square + 3.0 * fraction + 1.0) * (1.0 / 6.0),
        cubic_part * (1.0 / 6.0),
    )
    slopes = (
        -0.5 * remain * remain,
        (3.0 * square - 4.0 * fraction) * 0.5,
        (-3.0 * square + 2.0 * fraction + 1.0) * 0.5,
        0.5 * square,
    )
    return weights, slopes


def banded(place, terms):
    hits = [place == offset for offset in range(4)]

    def table(values):
        out = jnp.zeros(place.shape, jnp.float32)
        for hit, value in zip(hits, values):
            out = jnp.where(hit, jnp.broadcast_to(value, place.shape), out)
        return out

    return [table(values) for values in terms]


def row_numbers(rows):
    return lax.broadcasted_iota(jnp.int32, (rows, ATOMS), 0)


SHIFT_X = 53
SHIFT_XY = 57
EDGES = {0: 8, 1: 9, 7: -1}


def halo_x(lane):
    low = (lane == 15) | (lane == 4) | (lane == 8)
    upper = (lane == 0) | (lane == 5) | (lane == 9)
    top = (lane == 1) | (lane == 6) | (lane == 10)
    return jnp.where(low, -1, jnp.where(upper, 16, jnp.where(top, 17, 99)))


def halo_y(lane, j):
    before, behind = (j - 4) % 8, (j - 3) % 8
    choice = (
        ((lane <= 1) | (lane == 15), j),
        (lane == 4, before if before in EDGES else 99),
        ((lane == 5) | (lane == 6), behind if behind in EDGES else 99),
        (lane == 8, EDGES.get(before, 99)),
        ((lane == 9) | (lane == 10), EDGES.get(behind, 99)),
    )
    out = jnp.full(lane.shape, 99, jnp.int32)
    for mask, y in choice:
        out = jnp.where(mask, y, out)
    return out


def domain_tables(cells, fraction_ref):
    cell_x = jnp.right_shift(cells, 7) - 1
    cell_y = jnp.bitwise_and(jnp.right_shift(cells, 4), CY - 1) - 1
    terms_x = spline_terms(fraction_ref[0, 0])
    terms_y = spline_terms(fraction_ref[1, 0])
    lane = row_numbers(16)
    out = banded(lane - cell_x, terms_x) + banded(halo_x(lane) - cell_x, terms_x)
    out += banded(lane - 1 - cell_y, terms_y)
    for j in range(2, 7):
        out += banded(halo_y(lane, j) - cell_y, terms_y)
    return out


def message_blocks(tables):
    wx, dx, wx_halo, dx_halo, wy, dy = tables[:6]

    def row(y):
        return wy[y + 1 : y + 2], dy[y + 1 : y + 2]

    blocks = [(wx, dx) + row(m) for m in range(CY)]
    for j in range(8):
        if j in EDGES:
            blocks.append((wx, dx) + row(EDGES[j]))
        else:
            blocks.append((wx_halo, dx_halo, tables[2 + 2 * j], tables[3 + 2 * j]))
    return blocks


def rows_kernel(rows):
    rows[...] = natural(row_numbers(K))


def spread_kernel(
    rows, charge, fraction, base_cell, live_slot, force_cot, potential_cot, hartley,
    send, spectral, atoms, table_a, table_b, table_c,
):
    def store(field, value):
        for row in range(2):
            send[pl.ds(field * 2 * K + row, K, stride=2), :] = value[
                :, row * LANES : (row + 1) * LANES
            ]

    def transformed(first, table):
        value = split(product(hart, split(table)))
        spectral[first] = value[0]
        spectral[first + 1] = value[1]
        return value

    cells = base_cell[0]
    slot = lax.broadcasted_iota(jnp.int32, (1, ATOMS), 1)
    base_z = jnp.bitwise_and(slot, -16) + jnp.bitwise_and(cells, 15)
    place_z = jnp.bitwise_and(rows[...] - (base_z - 1), K - 1)
    wz, dz = banded(place_z, spline_terms(fraction[2, 0]))
    tables = domain_tables(cells, fraction)
    for index, value in enumerate(tables):
        atoms[index * 16 : (index + 1) * 16, :] = value
    live = live_slot[0].astype(jnp.float32)
    live_charge = charge[0] * live
    scalars = (live, live_charge, force_cot[0, 0], force_cot[1, 0], force_cot[2, 0])
    for row, value in enumerate(scalars):
        atoms[SCALARS + row : SCALARS + row + 1, :] = value
    atoms[SCALARS + 5 : SCALARS + 8, :] = jnp.zeros((3, ATOMS), jnp.float32)
    along_x = -live_charge * force_cot[0, 0]
    along_y = -live_charge * force_cot[1, 0]
    along_z = -live_charge * force_cot[2, 0]
    direct = live * potential_cot[0]
    for index, (wx, dx, wy, dy) in enumerate(message_blocks(tables)):
        rows = slice(index * 16, (index + 1) * 16)
        table_a[rows, :] = wx * (live_charge * wy)
        table_b[rows, :] = dx * (along_x * wy) + wx * (along_y * dy + direct * wy)
        table_c[rows, :] = wx * (along_z * wy)
    hart = (hartley[0], hartley[1])
    nt = ((1,), (1,))
    zw = transformed(0, wz)
    store(0, product(zw, split(table_a[...]), nt))
    zd = transformed(2, dz)
    store(1, product(zw, split(table_b[...]), nt) + product(zd, split(table_c[...]), nt))


def transposed_blocks(values):
    values = list(values)
    block = jnp.right_shift(lax.broadcasted_iota(jnp.int32, values[0].shape, 1), 4)
    for step in (1, 2, 4):
        upper = jnp.bitwise_and(block, step) != 0
        for i in range(8):
            if i & step == 0:
                first, second = values[i], values[i + step]
                values[i] = jnp.where(upper, pltpu.roll(second, 16 * step, 1), first)
                values[i + step] = jnp.where(upper, second, pltpu.roll(first, LANES - 16 * step, 1))
    return values


def plane_kernel(received, hartley, hartley_x, terms, send, plane):
    device = lax.axis_index("gx") * N_GY + lax.axis_index("gy")
    here = lax.broadcasted_iota(jnp.int32, (1, K), 1) == lax.rem(device, K)
    factor_x, square_x, factor_y, square_y = [terms[row : row + 1, :] for row in range(4)]
    factor_z = jnp.sum(jnp.where(here, factor_y, 0.0), axis=1, keepdims=True)
    square_z = jnp.sum(jnp.where(here, square_y, 0.0), axis=1, keepdims=True)
    hy = (hartley[0], hartley[1])
    hx = (hartley_x[0], hartley_x[1])
    place = lax.broadcasted_iota(jnp.int32, (N_GY, LANES), 1)
    block = jnp.right_shift(place, 4)
    lane = jnp.bitwise_and(place, 15)
    low = lane == 15
    high = lane <= 1
    last = block == 7
    first = block <= 1
    edge = last | first

    def rows(gx, half):
        return pl.ds(gx * 2 * N_GY + half, N_GY, stride=2)

    along_x, corners = [], []
    for gx in range(N_GX):
        halo = received[rows(gx, 1), :]
        along_x.append(jnp.where(edge, pltpu.roll(halo, LANES - SHIFT_X, 1), halo))
        corners.append(pltpu.roll(halo, LANES - SHIFT_XY, 1))

    def from_sides(values, gx):
        after, before = values[(gx + 1) % N_GX], values[gx - 1]
        return jnp.where(low, after, jnp.where(high, before, 0.0))

    folded = []
    for gx in range(N_GX):
        own = received[rows(gx, 0), :] + from_sides(along_x, gx)
        side = received[rows(gx, 1), :] + from_sides(corners, gx)
        after, before = pltpu.roll(side, N_GY - 1, 0), pltpu.roll(side, 1, 0)
        folded.append(own + jnp.where(last, after, jnp.where(first, before, 0.0)))
    for group in range(2):
        lines = transposed_blocks(folded[group * 8 : group * 8 + 8])
        for m, line in enumerate(lines):
            plane[m * N_GY : (m + 1) * N_GY, group * LANES : (group + 1) * LANES] = line
    half_way = product(split(plane[...]), hx)
    spectrum = product(hy, split(half_way))
    total_sq = jnp.transpose(square_y) + (square_x + square_z)
    factor = jnp.transpose(factor_y) * (factor_x * (factor_z * (1.0 / (math.pi * K))))
    kernel = jnp.where(total_sq > 0.0, factor / jnp.maximum(total_sq, 1.0), 0.0)
    half_way = product(hy, split(spectrum * kernel))
    plane[...] = product(split(half_way), hx)
    own = []
    for group in range(2):
        own += transposed_blocks(
            plane[m * N_GY : (m + 1) * N_GY, group * LANES : (group + 1) * LANES] for m in range(CY)
        )
    sides = [
        jnp.where(last, pltpu.roll(value, 1, 0), pltpu.roll(value, N_GY - 1, 0)) for value in own
    ]

    def to_sides(values, gx):
        return jnp.where(low, values[gx - 1], values[(gx + 1) % N_GX])

    turned_x = (lane >= 4) & (lane <= 6)
    turned_xy = (lane >= 8) & (lane <= 10)
    for gx in range(N_GX):
        cells_x = to_sides(own, gx)
        cells_xy = to_sides(sides, gx)
        halo = jnp.where(turned_x, pltpu.roll(cells_x, SHIFT_X, 1), cells_x)
        halo = jnp.where(turned_xy, pltpu.roll(cells_xy, SHIFT_XY, 1), halo)
        send[rows(gx, 0), :] = own[gx]
        send[rows(gx, 1), :] = jnp.where(edge, sides[gx], halo)


def sample_kernel(
    received, spectral, atoms, forces, potential, charge_grad, sample_a, sample_b, sample_c
):
    def field(index):
        halves = [received[pl.ds(index * 2 * K + half, K, stride=2), :] for half in range(2)]
        return split(jnp.concatenate(halves, axis=1).T)

    zw = (spectral[0], spectral[1])
    zd = (spectral[2], spectral[3])
    first = field(0)
    sample_a[...] = product(first, zw)
    sample_b[...] = product(first, zd)
    sample_c[...] = product(field(1), zw)
    live, live_charge, along_x, along_y, along_z = [
        atoms[SCALARS + row : SCALARS + row + 1, :] for row in range(5)
    ]
    tables = [atoms[index * 16 : (index + 1) * 16, :] for index in range(16)]
    sums = [jnp.zeros((16, ATOMS), jnp.float32) for _ in range(5)]
    for index, (wx, dx, wy, dy) in enumerate(message_blocks(tables)):
        rows = slice(index * 16, (index + 1) * 16)
        plain = sample_a[rows, :]
        plain_x = wx * plain
        sums[0] = sums[0] + plain_x * wy
        sums[1] = sums[1] + (dx * plain) * wy
        sums[2] = sums[2] + plain_x * dy
        sums[3] = sums[3] + (wx * sample_b[rows, :]) * wy
        sums[4] = sums[4] + (wx * sample_c[rows, :]) * wy
    mesh_value, grad_x, grad_y, grad_z, response = [
        jnp.sum(value, axis=0, keepdims=True) for value in sums
    ]
    forces[0, 0] = -live_charge * grad_x
    forces[1, 0] = -live_charge * grad_y
    forces[2, 0] = -live_charge * grad_z
    potential[0] = live * mesh_value
    charge_grad[0] = live * (response - along_x * grad_x - along_y * grad_y - along_z * grad_z)


def exchange(blocks):
    swapped = lax.all_to_all(
        blocks.reshape(DEVICES, 2, LANES), ("gx", "gy"), split_axis=0, concat_axis=0, tiled=True
    )
    return swapped.reshape(2 * DEVICES, LANES)


def on_device(charge, fraction, base_cell, live_slot, force_cot, potential_cot):
    y = plane_rows()
    freq = np.arange(K)
    hartley = split_table(cas_table(y, y))
    hartley_x = split_table(cas_table(freq, freq))
    factor, square = influence_factors()
    terms = np.zeros((8, K), np.float32)
    terms[:4] = factor, square, factor[y], square[y]
    params = pltpu.CompilerParams(vmem_limit_bytes=32 * 1024 * 1024)
    vmem = pl.BlockSpec(memory_space=pltpu.VMEM)
    f32 = jnp.float32
    table = pltpu.VMEM((K, ATOMS), f32)
    message = jax.ShapeDtypeStruct((2 * DEVICES, LANES), f32)
    arguments = (charge, fraction, base_cell, live_slot, force_cot, potential_cot)

    rows = pl.pallas_call(
        rows_kernel,
        out_shape=jax.ShapeDtypeStruct((K, ATOMS), jnp.int32),
        out_specs=vmem,
        compiler_params=params,
        cost_estimate=pl.CostEstimate(flops=10**9, bytes_accessed=10**6, transcendentals=0),
        name="rows",
    )()
    sent, spectral, atoms = pl.pallas_call(
        spread_kernel,
        out_shape=(
            message,
            jax.ShapeDtypeStruct((4, K, ATOMS), jnp.bfloat16),
            jax.ShapeDtypeStruct((SCALARS + 8, ATOMS), f32),
        ),
        in_specs=[vmem] * 8,
        out_specs=(vmem,) * 3,
        scratch_shapes=[table, table, table],
        compiler_params=params,
        name="spread",
    )(rows, *arguments, jnp.asarray(hartley))
    received = exchange(sent)
    solved = pl.pallas_call(
        plane_kernel,
        out_shape=message,
        in_specs=[vmem] * 4,
        out_specs=vmem,
        scratch_shapes=[pltpu.VMEM((K, K), f32)],
        compiler_params=params,
        name="plane",
    )(received, jnp.asarray(hartley), jnp.asarray(hartley_x), jnp.asarray(terms))
    returned = exchange(solved)
    return pl.pallas_call(
        sample_kernel,
        out_shape=(
            jax.ShapeDtypeStruct((3, 1, 1, ATOMS), f32),
            jax.ShapeDtypeStruct((1, 1, ATOMS), f32),
            jax.ShapeDtypeStruct((1, 1, ATOMS), f32),
        ),
        in_specs=[vmem] * 3,
        out_specs=(vmem, vmem, vmem),
        scratch_shapes=[table, table, table],
        compiler_params=params,
        name="sample",
    )(returned, spectral, atoms)


def solution(mesh):
    return jax.shard_map(
        on_device,
        mesh=mesh,
        in_specs=(
            P("gx", "gy", None),
            P(None, "gx", "gy", None),
            P("gx", "gy", None),
            P("gx", "gy", None),
            P(None, "gx", "gy", None),
            P("gx", "gy", None),
        ),
        out_specs=(P(None, "gx", "gy", None), P("gx", "gy", None), P("gx", "gy", None)),
        check_vma=False,
    )
```

```python
import math

import jax
import jax.numpy as jnp
import ml_dtypes
import numpy as np
from jax import lax
from jax.experimental import pallas as pl
from jax.experimental.pallas import tpu as pltpu
from jax.sharding import PartitionSpec as P

K = 256
CY = 8
N_GX = 16
N_GY = 32
ATOMS = 256
DEVICES = N_GX * N_GY
LANES = 128
SCALARS = 256

EWALD_SPLIT = 0.8


def cas_table(left, right):
    angles = 2.0 * math.pi / K * (left[:, None] * right[None, :] % K)
    return np.cos(angles) + np.sin(angles)


def split_table(table):
    high = table.astype(np.float32).astype(ml_dtypes.bfloat16)
    low = (table - high.astype(np.float64)).astype(np.float32).astype(ml_dtypes.bfloat16)
    return np.stack([high, low])


def plane_rows():
    m, gy = np.meshgrid(np.arange(CY), np.arange(N_GY), indexing="ij")
    return (gy * CY + m).reshape(-1)


def natural(index):
    return jnp.bitwise_or(
        jnp.left_shift(jnp.bitwise_and(index, N_GY - 1), 3), jnp.right_shift(index, 5)
    )


def influence_factors():
    freq = np.arange(K)
    nearest = np.minimum(freq, K - freq).astype(np.float64)
    damping = math.pi * math.pi / (EWALD_SPLIT * EWALD_SPLIT * K * K)
    cosine = np.cos(2.0 * math.pi / K * freq)
    factor = np.exp(-damping * nearest * nearest) * 9.0 / (2.0 + cosine) ** 2
    return factor.astype(np.float32), (nearest * nearest).astype(np.float32)


def split(value):
    high = value.astype(jnp.bfloat16)
    low = (value - high.astype(jnp.float32)).astype(jnp.bfloat16)
    return high, low


def product(left, right, dims=((1,), (0,))):
    def one(a, b):
        return lax.dot_general(a, b, (dims, ((), ())), preferred_element_type=jnp.float32)

    return one(left[0], right[0]) + (one(left[0], right[1]) + one(left[1], right[0]))


def spline_terms(fraction):
    square = fraction * fraction
    cubic_part = square * fraction
    remain = 1.0 - fraction
    weights = (
        remain * remain * remain * (1.0 / 6.0),
        (3.0 * cubic_part - 6.0 * square + 4.0) * (1.0 / 6.0),
        (-3.0 * cubic_part + 3.0 * square + 3.0 * fraction + 1.0) * (1.0 / 6.0),
        cubic_part * (1.0 / 6.0),
    )
    slopes = (
        -0.5 * remain * remain,
        (3.0 * square - 4.0 * fraction) * 0.5,
        (-3.0 * square + 2.0 * fraction + 1.0) * 0.5,
        0.5 * square,
    )
    return weights, slopes


def banded(place, terms):
    hits = [place == offset for offset in range(4)]

    def table(values):
        out = jnp.zeros(place.shape, jnp.float32)
        for hit, value in zip(hits, values):
            out = jnp.where(hit, jnp.broadcast_to(value, place.shape), out)
        return out

    return [table(values) for values in terms]


def row_numbers(rows):
    return lax.broadcasted_iota(jnp.int32, (rows, ATOMS), 0)


SHIFT_X = 53
SHIFT_XY = 57
EDGES = {0: 8, 1: 9, 7: -1}


def halo_x(lane):
    low = (lane == 15) | (lane == 4) | (lane == 8)
    upper = (lane == 0) | (lane == 5) | (lane == 9)
    top = (lane == 1) | (lane == 6) | (lane == 10)
    return jnp.where(low, -1, jnp.where(upper, 16, jnp.where(top, 17, 99)))


def halo_y(lane, j):
    before, behind = (j - 4) % 8, (j - 3) % 8
    choice = (
        ((lane <= 1) | (lane == 15), j),
        (lane == 4, before if before in EDGES else 99),
        ((lane == 5) | (lane == 6), behind if behind in EDGES else 99),
        (lane == 8, EDGES.get(before, 99)),
        ((lane == 9) | (lane == 10), EDGES.get(behind, 99)),
    )
    out = jnp.full(lane.shape, 99, jnp.int32)
    for mask, y in choice:
        out = jnp.where(mask, y, out)
    return out


def domain_tables(cells, fraction_ref):
    cell_x = jnp.right_shift(cells, 7) - 1
    cell_y = jnp.bitwise_and(jnp.right_shift(cells, 4), CY - 1) - 1
    terms_x = spline_terms(fraction_ref[0, 0])
    terms_y = spline_terms(fraction_ref[1, 0])
    lane = row_numbers(16)
    out = banded(lane - cell_x, terms_x) + banded(halo_x(lane) - cell_x, terms_x)
    out += banded(lane - 1 - cell_y, terms_y)
    for j in range(2, 7):
        out += banded(halo_y(lane, j) - cell_y, terms_y)
    return out


def message_blocks(tables):
    wx, dx, wx_halo, dx_halo, wy, dy = tables[:6]

    def row(y):
        return wy[y + 1 : y + 2], dy[y + 1 : y + 2]

    blocks = [(wx, dx) + row(m) for m in range(CY)]
    for j in range(8):
        if j in EDGES:
            blocks.append((wx, dx) + row(EDGES[j]))
        else:
            blocks.append((wx_halo, dx_halo, tables[2 + 2 * j], tables[3 + 2 * j]))
    return blocks


def rows_kernel(rows):
    rows[...] = natural(row_numbers(K))


def table_kernel(rows, hartley):
    cell = rows[...]
    frequency = natural(lax.broadcasted_iota(jnp.int32, (K, K), 1))
    turn = jnp.bitwise_and(cell * frequency + K // 8, K - 1) - K // 2
    quarter = jnp.where(turn > K // 4, K // 2 - turn, jnp.where(turn < -K // 4, -K // 2 - turn, turn))
    angle = quarter.astype(jnp.float32) * (2.0 * math.pi / K)
    square = angle * angle
    series = jnp.full((K, K), -1.0 / math.factorial(11), jnp.float32)
    for order in (9, 7, 5, 3, 1):
        series = series * square + (-1.0) ** (order // 2) / math.factorial(order)
    high, low = split(series * angle * -math.sqrt(2.0))
    hartley[0] = high
    hartley[1] = low


def spread_kernel(
    rows, charge, fraction, base_cell, live_slot, force_cot, potential_cot, hartley,
    send, spectral, atoms, table_a, table_b, table_c,
):
    def store(field, value):
        for row in range(2):
            send[pl.ds(field * 2 * K + row, K, stride=2), :] = value[
                :, row * LANES : (row + 1) * LANES
            ]

    def transformed(first, table):
        value = split(product(hart, split(table)))
        spectral[first] = value[0]
        spectral[first + 1] = value[1]
        return value

    cells = base_cell[0]
    slot = lax.broadcasted_iota(jnp.int32, (1, ATOMS), 1)
    base_z = jnp.bitwise_and(slot, -16) + jnp.bitwise_and(cells, 15)
    place_z = jnp.bitwise_and(rows[...] - (base_z - 1), K - 1)
    wz, dz = banded(place_z, spline_terms(fraction[2, 0]))
    tables = domain_tables(cells, fraction)
    for index, value in enumerate(tables):
        atoms[index * 16 : (index + 1) * 16, :] = value
    live = live_slot[0].astype(jnp.float32)
    live_charge = charge[0] * live
    scalars = (live, live_charge, force_cot[0, 0], force_cot[1, 0], force_cot[2, 0])
    for row, value in enumerate(scalars):
        atoms[SCALARS + row : SCALARS + row + 1, :] = value
    atoms[SCALARS + 5 : SCALARS + 8, :] = jnp.zeros((3, ATOMS), jnp.float32)
    along_x = -live_charge * force_cot[0, 0]
    along_y = -live_charge * force_cot[1, 0]
    along_z = -live_charge * force_cot[2, 0]
    direct = live * potential_cot[0]
    for index, (wx, dx, wy, dy) in enumerate(message_blocks(tables)):
        rows = slice(index * 16, (index + 1) * 16)
        table_a[rows, :] = wx * (live_charge * wy)
        table_b[rows, :] = dx * (along_x * wy) + wx * (along_y * dy + direct * wy)
        table_c[rows, :] = wx * (along_z * wy)
    hart = (hartley[0], hartley[1])
    nt = ((1,), (1,))
    zw = transformed(0, wz)
    zd = transformed(2, dz)
    store(0, product(zw, split(table_a[...]), nt))
    store(1, product(zw, split(table_b[...]), nt) + product(zd, split(table_c[...]), nt))


def transposed_blocks(values):
    values = list(values)
    block = jnp.right_shift(lax.broadcasted_iota(jnp.int32, values[0].shape, 1), 4)
    for step in (1, 2, 4):
        upper = jnp.bitwise_and(block, step) != 0
        for i in range(8):
            if i & step == 0:
                first, second = values[i], values[i + step]
                values[i] = jnp.where(upper, pltpu.roll(second, 16 * step, 1), first)
                values[i + step] = jnp.where(upper, second, pltpu.roll(first, LANES - 16 * step, 1))
    return values


def plane_kernel(received, hartley, hartley_x, terms, send, plane):
    device = lax.axis_index("gx") * N_GY + lax.axis_index("gy")
    here = lax.broadcasted_iota(jnp.int32, (1, K), 1) == lax.rem(device, K)
    factor_x, square_x, factor_y, square_y = [terms[row : row + 1, :] for row in range(4)]
    factor_z = jnp.sum(jnp.where(here, factor_y, 0.0), axis=1, keepdims=True)
    square_z = jnp.sum(jnp.where(here, square_y, 0.0), axis=1, keepdims=True)
    hy = (hartley[0], hartley[1])
    hx = (hartley_x[0], hartley_x[1])
    place = lax.broadcasted_iota(jnp.int32, (N_GY, LANES), 1)
    block = jnp.right_shift(place, 4)
    lane = jnp.bitwise_and(place, 15)
    low = lane == 15
    high = lane <= 1
    last = block == 7
    first = block <= 1
    edge = last | first

    def rows(gx, half):
        return pl.ds(gx * 2 * N_GY + half, N_GY, stride=2)

    along_x, corners = [], []
    for gx in range(N_GX):
        halo = received[rows(gx, 1), :]
        along_x.append(jnp.where(edge, pltpu.roll(halo, LANES - SHIFT_X, 1), halo))
        corners.append(pltpu.roll(halo, LANES - SHIFT_XY, 1))

    def from_sides(values, gx):
        after, before = values[(gx + 1) % N_GX], values[gx - 1]
        return jnp.where(low, after, jnp.where(high, before, 0.0))

    folded = []
    for gx in range(N_GX):
        own = received[rows(gx, 0), :] + from_sides(along_x, gx)
        side = received[rows(gx, 1), :] + from_sides(corners, gx)
        after, before = pltpu.roll(side, N_GY - 1, 0), pltpu.roll(side, 1, 0)
        folded.append(own + jnp.where(last, after, jnp.where(first, before, 0.0)))
    for group in range(2):
        lines = transposed_blocks(folded[group * 8 : group * 8 + 8])
        for m, line in enumerate(lines):
            plane[m * N_GY : (m + 1) * N_GY, group * LANES : (group + 1) * LANES] = line
    half_way = product(split(plane[...]), hx)
    spectrum = product(hy, split(half_way))
    total_sq = jnp.transpose(square_y) + (square_x + square_z)
    factor = jnp.transpose(factor_y) * (factor_x * (factor_z * (1.0 / (math.pi * K))))
    kernel = jnp.where(total_sq > 0.0, factor / jnp.maximum(total_sq, 1.0), 0.0)
    half_way = product(hy, split(spectrum * kernel))
    plane[...] = product(split(half_way), hx)
    own = []
    for group in range(2):
        own += transposed_blocks(
            plane[m * N_GY : (m + 1) * N_GY, group * LANES : (group + 1) * LANES] for m in range(CY)
        )
    sides = [
        jnp.where(last, pltpu.roll(value, 1, 0), pltpu.roll(value, N_GY - 1, 0)) for value in own
    ]

    def to_sides(values, gx):
        return jnp.where(low, values[gx - 1], values[(gx + 1) % N_GX])

    turned_x = (lane >= 4) & (lane <= 6)
    turned_xy = (lane >= 8) & (lane <= 10)
    for gx in range(N_GX):
        cells_x = to_sides(own, gx)
        cells_xy = to_sides(sides, gx)
        halo = jnp.where(turned_x, pltpu.roll(cells_x, SHIFT_X, 1), cells_x)
        halo = jnp.where(turned_xy, pltpu.roll(cells_xy, SHIFT_XY, 1), halo)
        send[rows(gx, 0), :] = own[gx]
        send[rows(gx, 1), :] = jnp.where(edge, sides[gx], halo)


def sample_kernel(
    received, spectral, atoms, forces, potential, charge_grad, sample_a, sample_b, sample_c
):
    def field(index):
        halves = [received[pl.ds(index * 2 * K + half, K, stride=2), :] for half in range(2)]
        return split(jnp.concatenate(halves, axis=1).T)

    zw = (spectral[0], spectral[1])
    zd = (spectral[2], spectral[3])
    first = field(0)
    sample_a[...] = product(first, zw)
    sample_b[...] = product(first, zd)
    sample_c[...] = product(field(1), zw)
    live, live_charge, along_x, along_y, along_z = [
        atoms[SCALARS + row : SCALARS + row + 1, :] for row in range(5)
    ]
    tables = [atoms[index * 16 : (index + 1) * 16, :] for index in range(16)]
    sums = [jnp.zeros((16, ATOMS), jnp.float32) for _ in range(5)]
    for index, (wx, dx, wy, dy) in enumerate(message_blocks(tables)):
        rows = slice(index * 16, (index + 1) * 16)
        plain = sample_a[rows, :]
        plain_x = wx * plain
        sums[0] = sums[0] + plain_x * wy
        sums[1] = sums[1] + (dx * plain) * wy
        sums[2] = sums[2] + plain_x * dy
        sums[3] = sums[3] + (wx * sample_b[rows, :]) * wy
        sums[4] = sums[4] + (wx * sample_c[rows, :]) * wy
    mesh_value, grad_x, grad_y, grad_z, response = [
        jnp.sum(value, axis=0, keepdims=True) for value in sums
    ]
    forces[0, 0] = -live_charge * grad_x
    forces[1, 0] = -live_charge * grad_y
    forces[2, 0] = -live_charge * grad_z
    potential[0] = live * mesh_value
    charge_grad[0] = live * (response - along_x * grad_x - along_y * grad_y - along_z * grad_z)


def exchange(blocks):
    swapped = lax.all_to_all(
        blocks.reshape(DEVICES, 2, LANES), ("gx", "gy"), split_axis=0, concat_axis=0, tiled=True
    )
    return swapped.reshape(2 * DEVICES, LANES)


def on_device(charge, fraction, base_cell, live_slot, force_cot, potential_cot):
    y = plane_rows()
    freq = np.arange(K)
    hartley_x = split_table(cas_table(freq, freq))
    factor, square = influence_factors()
    terms = np.zeros((8, K), np.float32)
    terms[:4] = factor, square, factor[y], square[y]
    params = pltpu.CompilerParams(vmem_limit_bytes=32 * 1024 * 1024)
    vmem = pl.BlockSpec(memory_space=pltpu.VMEM)
    f32 = jnp.float32
    table = pltpu.VMEM((K, ATOMS), f32)
    message = jax.ShapeDtypeStruct((2 * DEVICES, LANES), f32)
    arguments = (charge, fraction, base_cell, live_slot, force_cot, potential_cot)

    rows = pl.pallas_call(
        rows_kernel,
        out_shape=jax.ShapeDtypeStruct((K, ATOMS), jnp.int32),
        out_specs=vmem,
        compiler_params=params,
        cost_estimate=pl.CostEstimate(flops=10**9, bytes_accessed=10**6, transcendentals=0),
        name="rows",
    )()
    hartley = pl.pallas_call(
        table_kernel,
        out_shape=jax.ShapeDtypeStruct((2, K, K), jnp.bfloat16),
        in_specs=[vmem],
        out_specs=vmem,
        compiler_params=params,
        cost_estimate=pl.CostEstimate(flops=10**9, bytes_accessed=10**6, transcendentals=0),
        name="tables",
    )(rows)
    sent, spectral, atoms = pl.pallas_call(
        spread_kernel,
        out_shape=(
            message,
            jax.ShapeDtypeStruct((4, K, ATOMS), jnp.bfloat16),
            jax.ShapeDtypeStruct((SCALARS + 8, ATOMS), f32),
        ),
        in_specs=[vmem] * 8,
        out_specs=(vmem,) * 3,
        scratch_shapes=[table, table, table],
        compiler_params=params,
        name="spread",
    )(rows, *arguments, hartley)
    received = exchange(sent)
    solved = pl.pallas_call(
        plane_kernel,
        out_shape=message,
        in_specs=[vmem] * 4,
        out_specs=vmem,
        scratch_shapes=[pltpu.VMEM((K, K), f32)],
        compiler_params=params,
        name="plane",
    )(received, hartley, jnp.asarray(hartley_x), jnp.asarray(terms))
    returned = exchange(solved)
    return pl.pallas_call(
        sample_kernel,
        out_shape=(
            jax.ShapeDtypeStruct((3, 1, 1, ATOMS), f32),
            jax.ShapeDtypeStruct((1, 1, ATOMS), f32),
            jax.ShapeDtypeStruct((1, 1, ATOMS), f32),
        ),
        in_specs=[vmem] * 3,
        out_specs=(vmem, vmem, vmem),
        scratch_shapes=[table, table, table],
        compiler_params=params,
        name="sample",
    )(returned, spectral, atoms)


def solution(mesh):
    return jax.shard_map(
        on_device,
        mesh=mesh,
        in_specs=(
            P("gx", "gy", None),
            P(None, "gx", "gy", None),
            P("gx", "gy", None),
            P("gx", "gy", None),
            P(None, "gx", "gy", None),
            P("gx", "gy", None),
        ),
        out_specs=(P(None, "gx", "gy", None), P("gx", "gy", None), P("gx", "gy", None)),
        check_vma=False,
    )
```

```python
import math

import jax
import jax.numpy as jnp
import ml_dtypes
import numpy as np
from jax import lax
from jax.experimental import pallas as pl
from jax.experimental.pallas import tpu as pltpu
from jax.sharding import PartitionSpec as P

K = 256
CY = 8
N_GX = 16
N_GY = 32
ATOMS = 256
DEVICES = N_GX * N_GY
LANES = 128
SCALARS = 256

EWALD_SPLIT = 0.8


def cas_table(left, right):
    angles = 2.0 * math.pi / K * (left[:, None] * right[None, :] % K)
    return np.cos(angles) + np.sin(angles)


def split_table(table):
    high = table.astype(np.float32).astype(ml_dtypes.bfloat16)
    low = (table - high.astype(np.float64)).astype(np.float32).astype(ml_dtypes.bfloat16)
    return np.stack([high, low])


def plane_rows():
    m, gy = np.meshgrid(np.arange(CY), np.arange(N_GY), indexing="ij")
    return (gy * CY + m).reshape(-1)


def natural(index):
    return jnp.bitwise_or(
        jnp.left_shift(jnp.bitwise_and(index, N_GY - 1), 3), jnp.right_shift(index, 5)
    )


def influence_factors():
    freq = np.arange(K)
    nearest = np.minimum(freq, K - freq).astype(np.float64)
    damping = math.pi * math.pi / (EWALD_SPLIT * EWALD_SPLIT * K * K)
    cosine = np.cos(2.0 * math.pi / K * freq)
    factor = np.exp(-damping * nearest * nearest) * 9.0 / (2.0 + cosine) ** 2
    return factor.astype(np.float32), (nearest * nearest).astype(np.float32)


def split(value):
    high = value.astype(jnp.bfloat16)
    low = (value - high.astype(jnp.float32)).astype(jnp.bfloat16)
    return high, low


def product(left, right, dims=((1,), (0,))):
    def one(a, b):
        return lax.dot_general(a, b, (dims, ((), ())), preferred_element_type=jnp.float32)

    return one(left[0], right[0]) + (one(left[0], right[1]) + one(left[1], right[0]))


def spline_terms(fraction):
    square = fraction * fraction
    cubic_part = square * fraction
    remain = 1.0 - fraction
    weights = (
        remain * remain * remain * (1.0 / 6.0),
        (3.0 * cubic_part - 6.0 * square + 4.0) * (1.0 / 6.0),
        (-3.0 * cubic_part + 3.0 * square + 3.0 * fraction + 1.0) * (1.0 / 6.0),
        cubic_part * (1.0 / 6.0),
    )
    slopes = (
        -0.5 * remain * remain,
        (3.0 * square - 4.0 * fraction) * 0.5,
        (-3.0 * square + 2.0 * fraction + 1.0) * 0.5,
        0.5 * square,
    )
    return weights, slopes


def banded(place, terms):
    hits = [place == offset for offset in range(4)]

    def table(values):
        out = jnp.zeros(place.shape, jnp.float32)
        for hit, value in zip(hits, values):
            out = jnp.where(hit, jnp.broadcast_to(value, place.shape), out)
        return out

    return [table(values) for values in terms]


def row_numbers(rows):
    return lax.broadcasted_iota(jnp.int32, (rows, ATOMS), 0)


SHIFT_X = 53
SHIFT_XY = 57
EDGES = {0: 8, 1: 9, 7: -1}


def halo_x(lane):
    low = (lane == 15) | (lane == 4) | (lane == 8)
    upper = (lane == 0) | (lane == 5) | (lane == 9)
    top = (lane == 1) | (lane == 6) | (lane == 10)
    return jnp.where(low, -1, jnp.where(upper, 16, jnp.where(top, 17, 99)))


def halo_y(lane, j):
    before, behind = (j - 4) % 8, (j - 3) % 8
    choice = (
        ((lane <= 1) | (lane == 15), j),
        (lane == 4, before if before in EDGES else 99),
        ((lane == 5) | (lane == 6), behind if behind in EDGES else 99),
        (lane == 8, EDGES.get(before, 99)),
        ((lane == 9) | (lane == 10), EDGES.get(behind, 99)),
    )
    out = jnp.full(lane.shape, 99, jnp.int32)
    for mask, y in choice:
        out = jnp.where(mask, y, out)
    return out


def domain_tables(cells, fraction_ref):
    cell_x = jnp.right_shift(cells, 7) - 1
    cell_y = jnp.bitwise_and(jnp.right_shift(cells, 4), CY - 1) - 1
    terms_x = spline_terms(fraction_ref[0, 0])
    terms_y = spline_terms(fraction_ref[1, 0])
    lane = row_numbers(16)
    out = banded(lane - cell_x, terms_x) + banded(halo_x(lane) - cell_x, terms_x)
    out += banded(lane - 1 - cell_y, terms_y)
    for j in range(2, 7):
        out += banded(halo_y(lane, j) - cell_y, terms_y)
    return out


def message_blocks(tables):
    wx, dx, wx_halo, dx_halo, wy, dy = tables[:6]

    def row(y):
        return wy[y + 1 : y + 2], dy[y + 1 : y + 2]

    blocks = [(wx, dx) + row(m) for m in range(CY)]
    for j in range(8):
        if j in EDGES:
            blocks.append((wx, dx) + row(EDGES[j]))
        else:
            blocks.append((wx_halo, dx_halo, tables[2 + 2 * j], tables[3 + 2 * j]))
    return blocks


def rows_kernel(rows):
    rows[...] = natural(row_numbers(K))


def table_kernel(rows, hartley):
    cell = rows[...]
    frequency = natural(lax.broadcasted_iota(jnp.int32, (K, K), 1))
    turn = jnp.bitwise_and(cell * frequency + K // 8, K - 1) - K // 2
    quarter = jnp.where(turn > K // 4, K // 2 - turn, jnp.where(turn < -K // 4, -K // 2 - turn, turn))
    angle = quarter.astype(jnp.float32) * (2.0 * math.pi / K)
    square = angle * angle
    series = jnp.full((K, K), -1.0 / math.factorial(11), jnp.float32)
    for order in (9, 7, 5, 3, 1):
        series = series * square + (-1.0) ** (order // 2) / math.factorial(order)
    high, low = split(series * angle * -math.sqrt(2.0))
    hartley[0] = high
    hartley[1] = low


def spread_kernel(
    rows, charge, fraction, base_cell, live_slot, force_cot, potential_cot, hartley,
    send, spectral, atoms, table_a, table_b, table_c,
):
    def store(field, value):
        for row in range(2):
            send[pl.ds(field * 2 * K + row, K, stride=2), :] = value[
                :, row * LANES : (row + 1) * LANES
            ]

    def transformed(first, table):
        value = split(product(hart, split(table)))
        spectral[first] = value[0]
        spectral[first + 1] = value[1]
        return value

    cells = base_cell[0]
    slot = lax.broadcasted_iota(jnp.int32, (1, ATOMS), 1)
    base_z = jnp.bitwise_and(slot, -16) + jnp.bitwise_and(cells, 15)
    place_z = jnp.bitwise_and(rows[...] - (base_z - 1), K - 1)
    wz, dz = banded(place_z, spline_terms(fraction[2, 0]))
    tables = domain_tables(cells, fraction)
    for index, value in enumerate(tables):
        atoms[index * 16 : (index + 1) * 16, :] = value
    live = live_slot[0].astype(jnp.float32)
    live_charge = charge[0] * live
    scalars = (live, live_charge, force_cot[0, 0], force_cot[1, 0], force_cot[2, 0])
    for row, value in enumerate(scalars):
        atoms[SCALARS + row : SCALARS + row + 1, :] = value
    atoms[SCALARS + 5 : SCALARS + 8, :] = jnp.zeros((3, ATOMS), jnp.float32)
    along_x = -live_charge * force_cot[0, 0]
    along_y = -live_charge * force_cot[1, 0]
    along_z = -live_charge * force_cot[2, 0]
    direct = live * potential_cot[0]
    for index, (wx, dx, wy, dy) in enumerate(message_blocks(tables)):
        rows = slice(index * 16, (index + 1) * 16)
        table_a[rows, :] = wx * (live_charge * wy)
        table_b[rows, :] = dx * (along_x * wy) + wx * (along_y * dy + direct * wy)
        table_c[rows, :] = wx * (along_z * wy)
    hart = (hartley[0], hartley[1])
    nt = ((1,), (1,))
    zw = transformed(0, wz)
    zd = transformed(2, dz)
    store(0, product(zw, split(table_a[...]), nt))
    store(1, product(zw, split(table_b[...]), nt) + product(zd, split(table_c[...]), nt))


def transposed_blocks(values):
    values = list(values)
    block = jnp.right_shift(lax.broadcasted_iota(jnp.int32, values[0].shape, 1), 4)
    for step in (1, 2, 4):
        upper = jnp.bitwise_and(block, step) != 0
        for i in range(8):
            if i & step == 0:
                first, second = values[i], values[i + step]
                values[i] = jnp.where(upper, pltpu.roll(second, 16 * step, 1), first)
                values[i + step] = jnp.where(upper, second, pltpu.roll(first, LANES - 16 * step, 1))
    return values


def plane_kernel(received, hartley, hartley_x, terms, send):
    device = lax.axis_index("gx") * N_GY + lax.axis_index("gy")
    here = lax.broadcasted_iota(jnp.int32, (1, K), 1) == lax.rem(device, K)
    factor_x, square_x, factor_y, square_y = [terms[row : row + 1, :] for row in range(4)]
    factor_z = jnp.sum(jnp.where(here, factor_y, 0.0), axis=1, keepdims=True)
    square_z = jnp.sum(jnp.where(here, square_y, 0.0), axis=1, keepdims=True)
    hx = (hartley_x[0], hartley_x[1])
    place = lax.broadcasted_iota(jnp.int32, (N_GY, LANES), 1)
    block = jnp.right_shift(place, 4)
    lane = jnp.bitwise_and(place, 15)
    low = lane == 15
    high = lane <= 1
    last = block == 7
    first = block <= 1
    edge = last | first

    def rows(gx, half):
        return pl.ds(gx * 2 * N_GY + half, N_GY, stride=2)

    along_x, corners = [], []
    for gx in range(N_GX):
        halo = received[rows(gx, 1), :]
        along_x.append(jnp.where(edge, pltpu.roll(halo, LANES - SHIFT_X, 1), halo))
        corners.append(pltpu.roll(halo, LANES - SHIFT_XY, 1))

    def from_sides(values, gx):
        after, before = values[(gx + 1) % N_GX], values[gx - 1]
        return jnp.where(low, after, jnp.where(high, before, 0.0))

    folded = []
    for gx in range(N_GX):
        own = received[rows(gx, 0), :] + from_sides(along_x, gx)
        side = received[rows(gx, 1), :] + from_sides(corners, gx)
        after, before = pltpu.roll(side, N_GY - 1, 0), pltpu.roll(side, 1, 0)
        folded.append(own + jnp.where(last, after, jnp.where(first, before, 0.0)))
    groups = [transposed_blocks(folded[group * 8 : group * 8 + 8]) for group in range(2)]
    total_sq = jnp.transpose(square_y) + (square_x + square_z)
    factor = jnp.transpose(factor_y) * (factor_x * (factor_z * (1.0 / (math.pi * K))))
    kernel = jnp.where(total_sq > 0.0, factor / jnp.maximum(total_sq, 1.0), 0.0)
    cuts = slice(0, K // 2), slice(K // 2, K)
    hy = [(hartley[0, cut, :], hartley[1, cut, :]) for cut in cuts]

    def joined(blocks):
        return tuple(jnp.concatenate(pair, axis=0) for pair in zip(*blocks))

    lines = [
        jnp.concatenate([jnp.concatenate(group[m : m + 4], axis=0) for group in groups], axis=1)
        for m in (0, 4)
    ]
    half_way = joined([split(product(split(line), hx)) for line in lines])
    spectrum = [product(block, half_way) * kernel[cut] for block, cut in zip(hy, cuts)]
    spectrum = joined([split(block) for block in spectrum])
    half_way = [product(block, spectrum) for block in hy]
    solved = [product(split(block), hx) for block in half_way]
    own = []
    for group in range(2):
        lanes = slice(group * LANES, (group + 1) * LANES)
        own += transposed_blocks(
            solved[m // 4][m % 4 * N_GY : (m % 4 + 1) * N_GY, lanes] for m in range(CY)
        )
    sides = [
        jnp.where(last, pltpu.roll(value, 1, 0), pltpu.roll(value, N_GY - 1, 0)) for value in own
    ]

    def to_sides(values, gx):
        return jnp.where(low, values[gx - 1], values[(gx + 1) % N_GX])

    turned_x = (lane >= 4) & (lane <= 6)
    turned_xy = (lane >= 8) & (lane <= 10)
    for gx in range(N_GX):
        cells_x = to_sides(own, gx)
        cells_xy = to_sides(sides, gx)
        halo = jnp.where(turned_x, pltpu.roll(cells_x, SHIFT_X, 1), cells_x)
        halo = jnp.where(turned_xy, pltpu.roll(cells_xy, SHIFT_XY, 1), halo)
        send[rows(gx, 0), :] = own[gx]
        send[rows(gx, 1), :] = jnp.where(edge, sides[gx], halo)


def sample_kernel(
    received, spectral, atoms, forces, potential, charge_grad, sample_a, sample_b, sample_c
):
    def field(index):
        halves = [received[pl.ds(index * 2 * K + half, K, stride=2), :] for half in range(2)]
        return split(jnp.concatenate(halves, axis=1).T)

    zw = (spectral[0], spectral[1])
    zd = (spectral[2], spectral[3])
    first = field(0)
    sample_a[...] = product(first, zw)
    sample_b[...] = product(first, zd)
    sample_c[...] = product(field(1), zw)
    live, live_charge, along_x, along_y, along_z = [
        atoms[SCALARS + row : SCALARS + row + 1, :] for row in range(5)
    ]
    tables = [atoms[index * 16 : (index + 1) * 16, :] for index in range(16)]
    sums = [jnp.zeros((16, ATOMS), jnp.float32) for _ in range(5)]
    for index, (wx, dx, wy, dy) in enumerate(message_blocks(tables)):
        rows = slice(index * 16, (index + 1) * 16)
        plain = sample_a[rows, :]
        plain_x = wx * plain
        sums[0] = sums[0] + plain_x * wy
        sums[1] = sums[1] + (dx * plain) * wy
        sums[2] = sums[2] + plain_x * dy
        sums[3] = sums[3] + (wx * sample_b[rows, :]) * wy
        sums[4] = sums[4] + (wx * sample_c[rows, :]) * wy
    mesh_value, grad_x, grad_y, grad_z, response = [
        jnp.sum(value, axis=0, keepdims=True) for value in sums
    ]
    forces[0, 0] = -live_charge * grad_x
    forces[1, 0] = -live_charge * grad_y
    forces[2, 0] = -live_charge * grad_z
    potential[0] = live * mesh_value
    charge_grad[0] = live * (response - along_x * grad_x - along_y * grad_y - along_z * grad_z)


def exchange(blocks):
    swapped = lax.all_to_all(
        blocks.reshape(DEVICES, 2, LANES), ("gx", "gy"), split_axis=0, concat_axis=0, tiled=True
    )
    return swapped.reshape(2 * DEVICES, LANES)


def on_device(charge, fraction, base_cell, live_slot, force_cot, potential_cot):
    y = plane_rows()
    freq = np.arange(K)
    hartley_x = split_table(cas_table(freq, freq))
    factor, square = influence_factors()
    terms = np.zeros((8, K), np.float32)
    terms[:4] = factor, square, factor[y], square[y]
    params = pltpu.CompilerParams(vmem_limit_bytes=32 * 1024 * 1024)
    vmem = pl.BlockSpec(memory_space=pltpu.VMEM)
    f32 = jnp.float32
    table = pltpu.VMEM((K, ATOMS), f32)
    message = jax.ShapeDtypeStruct((2 * DEVICES, LANES), f32)
    arguments = (charge, fraction, base_cell, live_slot, force_cot, potential_cot)

    rows = pl.pallas_call(
        rows_kernel,
        out_shape=jax.ShapeDtypeStruct((K, ATOMS), jnp.int32),
        out_specs=vmem,
        compiler_params=params,
        cost_estimate=pl.CostEstimate(flops=10**9, bytes_accessed=10**6, transcendentals=0),
        name="rows",
    )()
    hartley = pl.pallas_call(
        table_kernel,
        out_shape=jax.ShapeDtypeStruct((2, K, K), jnp.bfloat16),
        in_specs=[vmem],
        out_specs=vmem,
        compiler_params=params,
        cost_estimate=pl.CostEstimate(flops=10**9, bytes_accessed=10**6, transcendentals=0),
        name="tables",
    )(rows)
    sent, spectral, atoms = pl.pallas_call(
        spread_kernel,
        out_shape=(
            message,
            jax.ShapeDtypeStruct((4, K, ATOMS), jnp.bfloat16),
            jax.ShapeDtypeStruct((SCALARS + 8, ATOMS), f32),
        ),
        in_specs=[vmem] * 8,
        out_specs=(vmem,) * 3,
        scratch_shapes=[table, table, table],
        compiler_params=params,
        name="spread",
    )(rows, *arguments, hartley)
    received = exchange(sent)
    solved = pl.pallas_call(
        plane_kernel,
        out_shape=message,
        in_specs=[vmem] * 4,
        out_specs=vmem,
        compiler_params=params,
        name="plane",
    )(received, hartley, jnp.asarray(hartley_x), jnp.asarray(terms))
    returned = exchange(solved)
    return pl.pallas_call(
        sample_kernel,
        out_shape=(
            jax.ShapeDtypeStruct((3, 1, 1, ATOMS), f32),
            jax.ShapeDtypeStruct((1, 1, ATOMS), f32),
            jax.ShapeDtypeStruct((1, 1, ATOMS), f32),
        ),
        in_specs=[vmem] * 3,
        out_specs=(vmem, vmem, vmem),
        scratch_shapes=[table, table, table],
        compiler_params=params,
        name="sample",
    )(returned, spectral, atoms)


def solution(mesh):
    return jax.shard_map(
        on_device,
        mesh=mesh,
        in_specs=(
            P("gx", "gy", None),
            P(None, "gx", "gy", None),
            P("gx", "gy", None),
            P("gx", "gy", None),
            P(None, "gx", "gy", None),
            P("gx", "gy", None),
        ),
        out_specs=(P(None, "gx", "gy", None), P("gx", "gy", None), P("gx", "gy", None)),
        check_vma=False,
    )
```

```python
import math

import jax
import jax.numpy as jnp
import ml_dtypes
import numpy as np
from jax import lax
from jax.experimental import pallas as pl
from jax.experimental.pallas import tpu as pltpu
from jax.sharding import PartitionSpec as P

K = 256
CY = 8
N_GX = 16
N_GY = 32
ATOMS = 256
DEVICES = N_GX * N_GY
LANES = 128
SCALARS = 256
HALVES = (slice(0, K // 2), slice(K // 2, K))

EWALD_SPLIT = 0.8


def cas_table(left, right):
    angles = 2.0 * math.pi / K * (left[:, None] * right[None, :] % K)
    return np.cos(angles) + np.sin(angles)


def split_table(table):
    high = table.astype(np.float32).astype(ml_dtypes.bfloat16)
    low = (table - high.astype(np.float64)).astype(np.float32).astype(ml_dtypes.bfloat16)
    return np.stack([high, low])


def plane_rows():
    m, gy = np.meshgrid(np.arange(CY), np.arange(N_GY), indexing="ij")
    return (gy * CY + m).reshape(-1)


def natural(index):
    return jnp.bitwise_or(
        jnp.left_shift(jnp.bitwise_and(index, N_GY - 1), 3), jnp.right_shift(index, 5)
    )


def influence_factors():
    freq = np.arange(K)
    nearest = np.minimum(freq, K - freq).astype(np.float64)
    damping = math.pi * math.pi / (EWALD_SPLIT * EWALD_SPLIT * K * K)
    cosine = np.cos(2.0 * math.pi / K * freq)
    factor = np.exp(-damping * nearest * nearest) * 9.0 / (2.0 + cosine) ** 2
    return factor.astype(np.float32), (nearest * nearest).astype(np.float32)


def split(value):
    high = value.astype(jnp.bfloat16)
    low = (value - high.astype(jnp.float32)).astype(jnp.bfloat16)
    return high, low


def product(left, right, dims=((1,), (0,))):
    def one(a, b):
        return lax.dot_general(a, b, (dims, ((), ())), preferred_element_type=jnp.float32)

    return one(left[0], right[0]) + (one(left[0], right[1]) + one(left[1], right[0]))


def joined(blocks):
    return tuple(jnp.concatenate(pair, axis=0) for pair in zip(*blocks))


def spline_terms(fraction):
    square = fraction * fraction
    cubic_part = square * fraction
    remain = 1.0 - fraction
    weights = (
        remain * remain * remain * (1.0 / 6.0),
        (3.0 * cubic_part - 6.0 * square + 4.0) * (1.0 / 6.0),
        (-3.0 * cubic_part + 3.0 * square + 3.0 * fraction + 1.0) * (1.0 / 6.0),
        cubic_part * (1.0 / 6.0),
    )
    slopes = (
        -0.5 * remain * remain,
        (3.0 * square - 4.0 * fraction) * 0.5,
        (-3.0 * square + 2.0 * fraction + 1.0) * 0.5,
        0.5 * square,
    )
    return weights, slopes


def banded(place, terms):
    hits = [place == offset for offset in range(4)]

    def table(values):
        out = jnp.zeros(place.shape, jnp.float32)
        for hit, value in zip(hits, values):
            out = jnp.where(hit, jnp.broadcast_to(value, place.shape), out)
        return out

    return [table(values) for values in terms]


def row_numbers(rows):
    return lax.broadcasted_iota(jnp.int32, (rows, ATOMS), 0)


SHIFT_X = 53
SHIFT_XY = 57
EDGES = {0: 8, 1: 9, 7: -1}


def halo_x(lane):
    low = (lane == 15) | (lane == 4) | (lane == 8)
    upper = (lane == 0) | (lane == 5) | (lane == 9)
    top = (lane == 1) | (lane == 6) | (lane == 10)
    return jnp.where(low, -1, jnp.where(upper, 16, jnp.where(top, 17, 99)))


def halo_y(lane, j):
    before, behind = (j - 4) % 8, (j - 3) % 8
    choice = (
        ((lane <= 1) | (lane == 15), j),
        (lane == 4, before if before in EDGES else 99),
        ((lane == 5) | (lane == 6), behind if behind in EDGES else 99),
        (lane == 8, EDGES.get(before, 99)),
        ((lane == 9) | (lane == 10), EDGES.get(behind, 99)),
    )
    out = jnp.full(lane.shape, 99, jnp.int32)
    for mask, y in choice:
        out = jnp.where(mask, y, out)
    return out


def domain_tables(cells, fraction_ref):
    cell_x = jnp.right_shift(cells, 7) - 1
    cell_y = jnp.bitwise_and(jnp.right_shift(cells, 4), CY - 1) - 1
    terms_x = spline_terms(fraction_ref[0, 0])
    terms_y = spline_terms(fraction_ref[1, 0])
    lane = row_numbers(16)
    out = banded(lane - cell_x, terms_x) + banded(halo_x(lane) - cell_x, terms_x)
    out += banded(lane - 1 - cell_y, terms_y)
    for j in range(2, 7):
        out += banded(halo_y(lane, j) - cell_y, terms_y)
    return out


def message_blocks(tables):
    wx, dx, wx_halo, dx_halo, wy, dy = tables[:6]

    def row(y):
        return wy[y + 1 : y + 2], dy[y + 1 : y + 2]

    blocks = [(wx, dx) + row(m) for m in range(CY)]
    for j in range(8):
        if j in EDGES:
            blocks.append((wx, dx) + row(EDGES[j]))
        else:
            blocks.append((wx_halo, dx_halo, tables[2 + 2 * j], tables[3 + 2 * j]))
    return blocks


def rows_kernel(rows):
    rows[...] = natural(row_numbers(K))


def table_kernel(rows, hartley):
    cell = rows[...]
    frequency = natural(lax.broadcasted_iota(jnp.int32, (K, K), 1))
    turn = jnp.bitwise_and(cell * frequency + K // 8, K - 1) - K // 2
    quarter = jnp.where(turn > K // 4, K // 2 - turn, jnp.where(turn < -K // 4, -K // 2 - turn, turn))
    angle = quarter.astype(jnp.float32) * (2.0 * math.pi / K)
    square = angle * angle
    series = jnp.full((K, K), -1.0 / math.factorial(11), jnp.float32)
    for order in (9, 7, 5, 3, 1):
        series = series * square + (-1.0) ** (order // 2) / math.factorial(order)
    high, low = split(series * angle * -math.sqrt(2.0))
    hartley[0] = high
    hartley[1] = low


def z_tables(rows, first, terms):
    zeros = [jnp.zeros((8, LANES), jnp.float32)] * 2
    halves = []
    for half in range(2):
        lanes = slice(half * LANES, (half + 1) * LANES)
        here = [[value[:, lanes] for value in values] for values in terms]

        def piece(start, count):
            place = rows[start : start + count, lanes] - first[:, lanes]
            return banded(jnp.bitwise_and(place, K - 1), here)

        pieces = []
        for m in range(CY):
            line = [piece(m * N_GY + half * 16, 16)]
            behind = piece(m * N_GY + (1 - half) * 16, 8) if m <= 2 else zeros
            before = piece(m * N_GY + (1 - half) * 16 + 8, 8) if m == 7 else zeros
            pieces += line + [behind, before] if half == 0 else [behind, before] + line
        halves.append([jnp.concatenate([part[i] for part in pieces], axis=0) for i in range(2)])
    return [jnp.concatenate([halves[0][i], halves[1][i]], axis=1) for i in range(2)]


def spread_kernel(
    rows, charge, fraction, base_cell, live_slot, force_cot, potential_cot, hartley,
    send, spectral, atoms, table_a, table_b, table_c,
):
    def store(field, value):
        for row in range(2):
            send[pl.ds(field * 2 * K + row, K, stride=2), :] = value[
                :, row * LANES : (row + 1) * LANES
            ]

    cells = base_cell[0]
    slot = lax.broadcasted_iota(jnp.int32, (1, ATOMS), 1)
    base_z = jnp.bitwise_and(slot, -16) + jnp.bitwise_and(cells, 15)
    wz, dz = z_tables(rows, base_z - 1, spline_terms(fraction[2, 0]))
    tables = domain_tables(cells, fraction)
    for index, value in enumerate(tables):
        atoms[index * 16 : (index + 1) * 16, :] = value
    live = live_slot[0].astype(jnp.float32)
    live_charge = charge[0] * live
    scalars = (live, live_charge, force_cot[0, 0], force_cot[1, 0], force_cot[2, 0])
    for row, value in enumerate(scalars):
        atoms[SCALARS + row : SCALARS + row + 1, :] = value
    atoms[SCALARS + 5 : SCALARS + 8, :] = jnp.zeros((3, ATOMS), jnp.float32)
    along_x = -live_charge * force_cot[0, 0]
    along_y = -live_charge * force_cot[1, 0]
    along_z = -live_charge * force_cot[2, 0]
    direct = live * potential_cot[0]
    for index, (wx, dx, wy, dy) in enumerate(message_blocks(tables)):
        rows = slice(index * 16, (index + 1) * 16)
        table_a[rows, :] = wx * (live_charge * wy)
        table_b[rows, :] = dx * (along_x * wy) + wx * (along_y * dy + direct * wy)
        table_c[rows, :] = wx * (along_z * wy)
    nt = ((1,), (1,))
    blocks = [(hartley[0, cut, :], hartley[1, cut, :]) for cut in HALVES]
    zw, zd = [
        joined([split(product(block, value)) for block in blocks]) for value in (split(wz), split(dz))
    ]
    for index, value in enumerate(zw + zd):
        spectral[index] = value
    store(0, product(zw, split(table_a[...]), nt))
    store(1, product(zw, split(table_b[...]), nt) + product(zd, split(table_c[...]), nt))


def transposed_blocks(values):
    values = list(values)
    block = jnp.right_shift(lax.broadcasted_iota(jnp.int32, values[0].shape, 1), 4)
    for step in (1, 2, 4):
        upper = jnp.bitwise_and(block, step) != 0
        for i in range(8):
            if i & step == 0:
                first, second = values[i], values[i + step]
                values[i] = jnp.where(upper, pltpu.roll(second, 16 * step, 1), first)
                values[i + step] = jnp.where(upper, second, pltpu.roll(first, LANES - 16 * step, 1))
    return values


def plane_kernel(received, hartley, hartley_x, terms, send):
    device = lax.axis_index("gx") * N_GY + lax.axis_index("gy")
    here = lax.broadcasted_iota(jnp.int32, (1, K), 1) == lax.rem(device, K)
    factor_x, square_x, factor_y, square_y = [terms[row : row + 1, :] for row in range(4)]
    factor_z = jnp.sum(jnp.where(here, factor_y, 0.0), axis=1, keepdims=True)
    square_z = jnp.sum(jnp.where(here, square_y, 0.0), axis=1, keepdims=True)
    hx = (hartley_x[0], hartley_x[1])
    place = lax.broadcasted_iota(jnp.int32, (N_GY, LANES), 1)
    block = jnp.right_shift(place, 4)
    lane = jnp.bitwise_and(place, 15)
    low = lane == 15
    high = lane <= 1
    last = block == 7
    first = block <= 1
    edge = last | first

    def rows(gx, half):
        return pl.ds(gx * 2 * N_GY + half, N_GY, stride=2)

    along_x, corners = [], []
    for gx in range(N_GX):
        halo = received[rows(gx, 1), :]
        along_x.append(jnp.where(edge, pltpu.roll(halo, LANES - SHIFT_X, 1), halo))
        corners.append(pltpu.roll(halo, LANES - SHIFT_XY, 1))

    def from_sides(values, gx):
        after, before = values[(gx + 1) % N_GX], values[gx - 1]
        return jnp.where(low, after, jnp.where(high, before, 0.0))

    folded = []
    for gx in range(N_GX):
        own = received[rows(gx, 0), :] + from_sides(along_x, gx)
        side = received[rows(gx, 1), :] + from_sides(corners, gx)
        after, before = pltpu.roll(side, N_GY - 1, 0), pltpu.roll(side, 1, 0)
        folded.append(own + jnp.where(last, after, jnp.where(first, before, 0.0)))
    groups = [transposed_blocks(folded[group * 8 : group * 8 + 8]) for group in range(2)]
    total_sq = jnp.transpose(square_y) + (square_x + square_z)
    factor = jnp.transpose(factor_y) * (factor_x * (factor_z * (1.0 / (math.pi * K))))
    kernel = jnp.where(total_sq > 0.0, factor / jnp.maximum(total_sq, 1.0), 0.0)
    hy = [(hartley[0, cut, :], hartley[1, cut, :]) for cut in HALVES]
    lines = [
        jnp.concatenate([jnp.concatenate(group[m : m + 4], axis=0) for group in groups], axis=1)
        for m in (0, 4)
    ]
    half_way = joined([split(product(split(line), hx)) for line in lines])
    spectrum = [product(block, half_way) * kernel[cut] for block, cut in zip(hy, HALVES)]
    spectrum = joined([split(block) for block in spectrum])
    half_way = [product(block, spectrum) for block in hy]
    solved = [product(split(block), hx) for block in half_way]
    own = []
    for group in range(2):
        lanes = slice(group * LANES, (group + 1) * LANES)
        own += transposed_blocks(
            solved[m // 4][m % 4 * N_GY : (m % 4 + 1) * N_GY, lanes] for m in range(CY)
        )
    sides = [
        jnp.where(last, pltpu.roll(value, 1, 0), pltpu.roll(value, N_GY - 1, 0)) for value in own
    ]

    def to_sides(values, gx):
        return jnp.where(low, values[gx - 1], values[(gx + 1) % N_GX])

    turned_x = (lane >= 4) & (lane <= 6)
    turned_xy = (lane >= 8) & (lane <= 10)
    for gx in range(N_GX):
        cells_x = to_sides(own, gx)
        cells_xy = to_sides(sides, gx)
        halo = jnp.where(turned_x, pltpu.roll(cells_x, SHIFT_X, 1), cells_x)
        halo = jnp.where(turned_xy, pltpu.roll(cells_xy, SHIFT_XY, 1), halo)
        send[rows(gx, 0), :] = own[gx]
        send[rows(gx, 1), :] = jnp.where(edge, sides[gx], halo)


def sample_kernel(
    received, spectral, atoms, forces, potential, charge_grad, sample_a, sample_b, sample_c
):
    def field(index):
        halves = [received[pl.ds(index * 2 * K + half, K, stride=2), :] for half in range(2)]
        return split(jnp.concatenate(halves, axis=1).T)

    zw = (spectral[0], spectral[1])
    zd = (spectral[2], spectral[3])
    first = field(0)
    sample_a[...] = product(first, zw)
    sample_b[...] = product(first, zd)
    sample_c[...] = product(field(1), zw)
    live, live_charge, along_x, along_y, along_z = [
        atoms[SCALARS + row : SCALARS + row + 1, :] for row in range(5)
    ]
    tables = [atoms[index * 16 : (index + 1) * 16, :] for index in range(16)]
    sums = [jnp.zeros((16, ATOMS), jnp.float32) for _ in range(5)]
    for index, (wx, dx, wy, dy) in enumerate(message_blocks(tables)):
        rows = slice(index * 16, (index + 1) * 16)
        plain = sample_a[rows, :]
        plain_x = wx * plain
        sums[0] = sums[0] + plain_x * wy
        sums[1] = sums[1] + (dx * plain) * wy
        sums[2] = sums[2] + plain_x * dy
        sums[3] = sums[3] + (wx * sample_b[rows, :]) * wy
        sums[4] = sums[4] + (wx * sample_c[rows, :]) * wy
    mesh_value, grad_x, grad_y, grad_z, response = [
        jnp.sum(value, axis=0, keepdims=True) for value in sums
    ]
    forces[0, 0] = -live_charge * grad_x
    forces[1, 0] = -live_charge * grad_y
    forces[2, 0] = -live_charge * grad_z
    potential[0] = live * mesh_value
    charge_grad[0] = live * (response - along_x * grad_x - along_y * grad_y - along_z * grad_z)


def exchange(blocks):
    swapped = lax.all_to_all(
        blocks.reshape(DEVICES, 2, LANES), ("gx", "gy"), split_axis=0, concat_axis=0, tiled=True
    )
    return swapped.reshape(2 * DEVICES, LANES)


def on_device(charge, fraction, base_cell, live_slot, force_cot, potential_cot):
    y = plane_rows()
    freq = np.arange(K)
    hartley_x = split_table(cas_table(freq, freq))
    factor, square = influence_factors()
    terms = np.zeros((8, K), np.float32)
    terms[:4] = factor, square, factor[y], square[y]
    params = pltpu.CompilerParams(vmem_limit_bytes=32 * 1024 * 1024)
    vmem = pl.BlockSpec(memory_space=pltpu.VMEM)
    f32 = jnp.float32
    table = pltpu.VMEM((K, ATOMS), f32)
    message = jax.ShapeDtypeStruct((2 * DEVICES, LANES), f32)
    arguments = (charge, fraction, base_cell, live_slot, force_cot, potential_cot)

    rows = pl.pallas_call(
        rows_kernel,
        out_shape=jax.ShapeDtypeStruct((K, ATOMS), jnp.int32),
        out_specs=vmem,
        compiler_params=params,
        cost_estimate=pl.CostEstimate(flops=10**9, bytes_accessed=10**6, transcendentals=0),
        name="rows",
    )()
    hartley = pl.pallas_call(
        table_kernel,
        out_shape=jax.ShapeDtypeStruct((2, K, K), jnp.bfloat16),
        in_specs=[vmem],
        out_specs=vmem,
        compiler_params=params,
        cost_estimate=pl.CostEstimate(flops=10**9, bytes_accessed=10**6, transcendentals=0),
        name="tables",
    )(rows)
    sent, spectral, atoms = pl.pallas_call(
        spread_kernel,
        out_shape=(
            message,
            jax.ShapeDtypeStruct((4, K, ATOMS), jnp.bfloat16),
            jax.ShapeDtypeStruct((SCALARS + 8, ATOMS), f32),
        ),
        in_specs=[vmem] * 8,
        out_specs=(vmem,) * 3,
        scratch_shapes=[table, table, table],
        compiler_params=params,
        name="spread",
    )(rows, *arguments, hartley)
    received = exchange(sent)
    solved = pl.pallas_call(
        plane_kernel,
        out_shape=message,
        in_specs=[vmem] * 4,
        out_specs=vmem,
        compiler_params=params,
        name="plane",
    )(received, hartley, jnp.asarray(hartley_x), jnp.asarray(terms))
    returned = exchange(solved)
    return pl.pallas_call(
        sample_kernel,
        out_shape=(
            jax.ShapeDtypeStruct((3, 1, 1, ATOMS), f32),
            jax.ShapeDtypeStruct((1, 1, ATOMS), f32),
            jax.ShapeDtypeStruct((1, 1, ATOMS), f32),
        ),
        in_specs=[vmem] * 3,
        out_specs=(vmem, vmem, vmem),
        scratch_shapes=[table, table, table],
        compiler_params=params,
        name="sample",
    )(returned, spectral, atoms)


def solution(mesh):
    return jax.shard_map(
        on_device,
        mesh=mesh,
        in_specs=(
            P("gx", "gy", None),
            P(None, "gx", "gy", None),
            P("gx", "gy", None),
            P("gx", "gy", None),
            P(None, "gx", "gy", None),
            P("gx", "gy", None),
        ),
        out_specs=(P(None, "gx", "gy", None), P("gx", "gy", None), P("gx", "gy", None)),
        check_vma=False,
    )
```

```python
import math

import jax
import jax.numpy as jnp
import ml_dtypes
import numpy as np
from jax import lax
from jax.experimental import pallas as pl
from jax.experimental.pallas import tpu as pltpu
from jax.sharding import PartitionSpec as P

K = 256
CY = 8
N_GX = 16
N_GY = 32
ATOMS = 256
DEVICES = N_GX * N_GY
LANES = 128
SCALARS = 256
HALVES = (slice(0, K // 2), slice(K // 2, K))

EWALD_SPLIT = 0.8


def cas_table(left, right):
    angles = 2.0 * math.pi / K * (left[:, None] * right[None, :] % K)
    return np.cos(angles) + np.sin(angles)


def split_table(table):
    high = table.astype(np.float32).astype(ml_dtypes.bfloat16)
    low = (table - high.astype(np.float64)).astype(np.float32).astype(ml_dtypes.bfloat16)
    return np.stack([high, low])


def plane_rows():
    m, gy = np.meshgrid(np.arange(CY), np.arange(N_GY), indexing="ij")
    return (gy * CY + m).reshape(-1)


def natural(index):
    return jnp.bitwise_or(
        jnp.left_shift(jnp.bitwise_and(index, N_GY - 1), 3), jnp.right_shift(index, 5)
    )


def influence_factors():
    freq = np.arange(K)
    nearest = np.minimum(freq, K - freq).astype(np.float64)
    damping = math.pi * math.pi / (EWALD_SPLIT * EWALD_SPLIT * K * K)
    cosine = np.cos(2.0 * math.pi / K * freq)
    factor = np.exp(-damping * nearest * nearest) * 9.0 / (2.0 + cosine) ** 2
    return factor.astype(np.float32), (nearest * nearest).astype(np.float32)


def split(value):
    high = value.astype(jnp.bfloat16)
    low = (value - high.astype(jnp.float32)).astype(jnp.bfloat16)
    return high, low


def product(left, right, dims=((1,), (0,))):
    def one(a, b):
        return lax.dot_general(a, b, (dims, ((), ())), preferred_element_type=jnp.float32)

    return one(left[0], right[0]) + (one(left[0], right[1]) + one(left[1], right[0]))


def joined(blocks):
    return tuple(jnp.concatenate(pair, axis=0) for pair in zip(*blocks))


def spline_terms(fraction):
    square = fraction * fraction
    cubic_part = square * fraction
    remain = 1.0 - fraction
    weights = (
        remain * remain * remain * (1.0 / 6.0),
        (3.0 * cubic_part - 6.0 * square + 4.0) * (1.0 / 6.0),
        (-3.0 * cubic_part + 3.0 * square + 3.0 * fraction + 1.0) * (1.0 / 6.0),
        cubic_part * (1.0 / 6.0),
    )
    slopes = (
        -0.5 * remain * remain,
        (3.0 * square - 4.0 * fraction) * 0.5,
        (-3.0 * square + 2.0 * fraction + 1.0) * 0.5,
        0.5 * square,
    )
    return weights, slopes


def banded(place, terms):
    hits = [place == offset for offset in range(4)]

    def table(values):
        out = jnp.zeros(place.shape, jnp.float32)
        for hit, value in zip(hits, values):
            out = jnp.where(hit, jnp.broadcast_to(value, place.shape), out)
        return out

    return [table(values) for values in terms]


def row_numbers(rows):
    return lax.broadcasted_iota(jnp.int32, (rows, ATOMS), 0)


SHIFT_X = 53
SHIFT_XY = 57
EDGES = {0: 8, 1: 9, 7: -1}


def halo_x(lane):
    low = (lane == 15) | (lane == 4) | (lane == 8)
    upper = (lane == 0) | (lane == 5) | (lane == 9)
    top = (lane == 1) | (lane == 6) | (lane == 10)
    return jnp.where(low, -1, jnp.where(upper, 16, jnp.where(top, 17, 99)))


def halo_y(lane, j):
    before, behind = (j - 4) % 8, (j - 3) % 8
    choice = (
        ((lane <= 1) | (lane == 15), j),
        (lane == 4, before if before in EDGES else 99),
        ((lane == 5) | (lane == 6), behind if behind in EDGES else 99),
        (lane == 8, EDGES.get(before, 99)),
        ((lane == 9) | (lane == 10), EDGES.get(behind, 99)),
    )
    out = jnp.full(lane.shape, 99, jnp.int32)
    for mask, y in choice:
        out = jnp.where(mask, y, out)
    return out


def domain_tables(cells, fraction_ref):
    cell_x = jnp.right_shift(cells, 7) - 1
    cell_y = jnp.bitwise_and(jnp.right_shift(cells, 4), CY - 1) - 1
    terms_x = spline_terms(fraction_ref[0, 0])
    terms_y = spline_terms(fraction_ref[1, 0])
    lane = row_numbers(16)
    out = banded(lane - cell_x, terms_x) + banded(halo_x(lane) - cell_x, terms_x)
    out += banded(lane - 1 - cell_y, terms_y)
    for j in range(2, 7):
        out += banded(halo_y(lane, j) - cell_y, terms_y)
    return out


def message_blocks(tables):
    wx, dx, wx_halo, dx_halo, wy, dy = tables[:6]

    def row(y):
        return wy[y + 1 : y + 2], dy[y + 1 : y + 2]

    blocks = [(wx, dx) + row(m) for m in range(CY)]
    for j in range(8):
        if j in EDGES:
            blocks.append((wx, dx) + row(EDGES[j]))
        else:
            blocks.append((wx_halo, dx_halo, tables[2 + 2 * j], tables[3 + 2 * j]))
    return blocks


def rows_kernel(rows):
    rows[...] = natural(row_numbers(K))


def table_kernel(rows, hartley):
    cell = rows[...]
    frequency = natural(lax.broadcasted_iota(jnp.int32, (K, K), 1))
    turn = jnp.bitwise_and(cell * frequency + K // 8, K - 1) - K // 2
    quarter = jnp.where(turn > K // 4, K // 2 - turn, jnp.where(turn < -K // 4, -K // 2 - turn, turn))
    angle = quarter.astype(jnp.float32) * (2.0 * math.pi / K)
    square = angle * angle
    series = jnp.full((K, K), -1.0 / math.factorial(11), jnp.float32)
    for order in (9, 7, 5, 3, 1):
        series = series * square + (-1.0) ** (order // 2) / math.factorial(order)
    high, low = split(series * angle * -math.sqrt(2.0))
    hartley[0] = high
    hartley[1] = low


def z_tables(rows, first, terms):
    zeros = [jnp.zeros((8, LANES), jnp.float32)] * 2
    halves = []
    for half in range(2):
        lanes = slice(half * LANES, (half + 1) * LANES)
        here = [[value[:, lanes] for value in values] for values in terms]

        def piece(start, count):
            place = rows[start : start + count, lanes] - first[:, lanes]
            return banded(jnp.bitwise_and(place, K - 1), here)

        pieces = []
        for m in range(CY):
            line = [piece(m * N_GY + half * 16, 16)]
            behind = piece(m * N_GY + (1 - half) * 16, 8) if m <= 2 else zeros
            before = piece(m * N_GY + (1 - half) * 16 + 8, 8) if m == 7 else zeros
            pieces += line + [behind, before] if half == 0 else [behind, before] + line
        halves.append([jnp.concatenate([part[i] for part in pieces], axis=0) for i in range(2)])
    return [jnp.concatenate([halves[0][i], halves[1][i]], axis=1) for i in range(2)]


def spread_kernel(
    rows, charge, fraction, base_cell, live_slot, force_cot, potential_cot, hartley,
    send, spectral, atoms, table_a, table_b, table_c,
):
    def store(field, value):
        for row in range(2):
            send[pl.ds(field * 2 * K + row, K, stride=2), :] = value[
                :, row * LANES : (row + 1) * LANES
            ]

    cells = base_cell[0]
    slot = lax.broadcasted_iota(jnp.int32, (1, ATOMS), 1)
    base_z = jnp.bitwise_and(slot, -16) + jnp.bitwise_and(cells, 15)
    wz, dz = z_tables(rows, base_z - 1, spline_terms(fraction[2, 0]))
    tables = domain_tables(cells, fraction)
    for index, value in enumerate(tables):
        atoms[index * 16 : (index + 1) * 16, :] = value
    live = live_slot[0].astype(jnp.float32)
    live_charge = charge[0] * live
    scalars = (live, live_charge, force_cot[0, 0], force_cot[1, 0], force_cot[2, 0])
    for row, value in enumerate(scalars):
        atoms[SCALARS + row : SCALARS + row + 1, :] = value
    atoms[SCALARS + 5 : SCALARS + 8, :] = jnp.zeros((3, ATOMS), jnp.float32)
    along_x = -live_charge * force_cot[0, 0]
    along_y = -live_charge * force_cot[1, 0]
    along_z = -live_charge * force_cot[2, 0]
    direct = live * potential_cot[0]
    for index, (wx, dx, wy, dy) in enumerate(message_blocks(tables)):
        rows = slice(index * 16, (index + 1) * 16)
        table_a[rows, :] = wx * (live_charge * wy)
        table_b[rows, :] = dx * (along_x * wy) + wx * (along_y * dy + direct * wy)
        table_c[rows, :] = wx * (along_z * wy)
    nt = ((1,), (1,))
    blocks = [(hartley[0, cut, :], hartley[1, cut, :]) for cut in HALVES]
    zw, zd = [
        joined([split(product(block, value)) for block in blocks]) for value in (split(wz), split(dz))
    ]
    for index, value in enumerate(zw + zd):
        spectral[index] = value
    store(0, product(zw, split(table_a[...]), nt))
    store(1, product(zw, split(table_b[...]), nt) + product(zd, split(table_c[...]), nt))


def exchanged(values, steps, members):
    block = jnp.right_shift(lax.broadcasted_iota(jnp.int32, values[members[0]].shape, 1), 4)
    for step in steps:
        upper = jnp.bitwise_and(block, step) != 0
        for i in members:
            if i & step == 0:
                first, second = values[i], values[i + step]
                values[i] = jnp.where(upper, pltpu.roll(second, 16 * step, 1), first)
                values[i + step] = jnp.where(upper, second, pltpu.roll(first, LANES - 16 * step, 1))


def transposed_blocks(values):
    values = list(values)
    exchanged(values, (1, 2, 4), range(8))
    return values


def plane_kernel(received, hartley, hartley_x, terms, send):
    device = lax.axis_index("gx") * N_GY + lax.axis_index("gy")
    here = lax.broadcasted_iota(jnp.int32, (1, K), 1) == lax.rem(device, K)
    factor_x, square_x, factor_y, square_y = [terms[row : row + 1, :] for row in range(4)]
    factor_z = jnp.sum(jnp.where(here, factor_y, 0.0), axis=1, keepdims=True)
    square_z = jnp.sum(jnp.where(here, square_y, 0.0), axis=1, keepdims=True)
    hx = (hartley_x[0], hartley_x[1])
    place = lax.broadcasted_iota(jnp.int32, (N_GY, LANES), 1)
    block = jnp.right_shift(place, 4)
    lane = jnp.bitwise_and(place, 15)
    low = lane == 15
    high = lane <= 1
    last = block == 7
    first = block <= 1
    edge = last | first

    def rows(gx, half):
        return pl.ds(gx * 2 * N_GY + half, N_GY, stride=2)

    along_x, corners = [], []
    for gx in range(N_GX):
        halo = received[rows(gx, 1), :]
        along_x.append(jnp.where(edge, pltpu.roll(halo, LANES - SHIFT_X, 1), halo))
        corners.append(pltpu.roll(halo, LANES - SHIFT_XY, 1))

    def from_sides(values, gx):
        after, before = values[(gx + 1) % N_GX], values[gx - 1]
        return jnp.where(low, after, jnp.where(high, before, 0.0))

    folded = []
    for gx in range(N_GX):
        own = received[rows(gx, 0), :] + from_sides(along_x, gx)
        side = received[rows(gx, 1), :] + from_sides(corners, gx)
        after, before = pltpu.roll(side, N_GY - 1, 0), pltpu.roll(side, 1, 0)
        folded.append(own + jnp.where(last, after, jnp.where(first, before, 0.0)))
    total_sq = jnp.transpose(square_y) + (square_x + square_z)
    factor = jnp.transpose(factor_y) * (factor_x * (factor_z * (1.0 / (math.pi * K))))
    kernel = jnp.where(total_sq > 0.0, factor / jnp.maximum(total_sq, 1.0), 0.0)
    hy = [(hartley[0, cut, :], hartley[1, cut, :]) for cut in HALVES]
    groups = [folded[0:8], folded[8:16]]
    for group in groups:
        exchanged(group, (4,), range(8))
    lines = []
    for low_line in (0, 4):
        members = range(low_line, low_line + 4)
        for group in groups:
            exchanged(group, (2, 1), members)
        line = [jnp.concatenate([group[m] for m in members], axis=0) for group in groups]
        lines.append(split(product(split(jnp.concatenate(line, axis=1)), hx)))
    half_way = joined(lines)
    spectrum = [product(block, half_way) * kernel[cut] for block, cut in zip(hy, HALVES)]
    spectrum = joined([split(block) for block in spectrum])
    half_way = [product(block, spectrum) for block in hy]
    solved = [product(split(block), hx) for block in half_way]
    own = []
    for group in range(2):
        lanes = slice(group * LANES, (group + 1) * LANES)
        own += transposed_blocks(
            solved[m // 4][m % 4 * N_GY : (m % 4 + 1) * N_GY, lanes] for m in range(CY)
        )
    sides = [
        jnp.where(last, pltpu.roll(value, 1, 0), pltpu.roll(value, N_GY - 1, 0)) for value in own
    ]

    def to_sides(values, gx):
        return jnp.where(low, values[gx - 1], values[(gx + 1) % N_GX])

    turned_x = (lane >= 4) & (lane <= 6)
    turned_xy = (lane >= 8) & (lane <= 10)
    for gx in range(N_GX):
        cells_x = to_sides(own, gx)
        cells_xy = to_sides(sides, gx)
        halo = jnp.where(turned_x, pltpu.roll(cells_x, SHIFT_X, 1), cells_x)
        halo = jnp.where(turned_xy, pltpu.roll(cells_xy, SHIFT_XY, 1), halo)
        send[rows(gx, 0), :] = own[gx]
        send[rows(gx, 1), :] = jnp.where(edge, sides[gx], halo)


def sample_kernel(
    received, spectral, atoms, forces, potential, charge_grad, sample_a, sample_b, sample_c
):
    def field(index):
        halves = [received[pl.ds(index * 2 * K + half, K, stride=2), :] for half in range(2)]
        return split(jnp.concatenate(halves, axis=1).T)

    zw = (spectral[0], spectral[1])
    zd = (spectral[2], spectral[3])
    first = field(0)
    sample_a[...] = product(first, zw)
    sample_b[...] = product(first, zd)
    sample_c[...] = product(field(1), zw)
    live, live_charge, along_x, along_y, along_z = [
        atoms[SCALARS + row : SCALARS + row + 1, :] for row in range(5)
    ]
    tables = [atoms[index * 16 : (index + 1) * 16, :] for index in range(16)]
    sums = [jnp.zeros((16, ATOMS), jnp.float32) for _ in range(5)]
    for index, (wx, dx, wy, dy) in enumerate(message_blocks(tables)):
        rows = slice(index * 16, (index + 1) * 16)
        plain = sample_a[rows, :]
        plain_x = wx * plain
        sums[0] = sums[0] + plain_x * wy
        sums[1] = sums[1] + (dx * plain) * wy
        sums[2] = sums[2] + plain_x * dy
        sums[3] = sums[3] + (wx * sample_b[rows, :]) * wy
        sums[4] = sums[4] + (wx * sample_c[rows, :]) * wy
    mesh_value, grad_x, grad_y, grad_z, response = [
        jnp.sum(value, axis=0, keepdims=True) for value in sums
    ]
    forces[0, 0] = -live_charge * grad_x
    forces[1, 0] = -live_charge * grad_y
    forces[2, 0] = -live_charge * grad_z
    potential[0] = live * mesh_value
    charge_grad[0] = live * (response - along_x * grad_x - along_y * grad_y - along_z * grad_z)


def exchange(blocks):
    swapped = lax.all_to_all(
        blocks.reshape(DEVICES, 2, LANES), ("gx", "gy"), split_axis=0, concat_axis=0, tiled=True
    )
    return swapped.reshape(2 * DEVICES, LANES)


def on_device(charge, fraction, base_cell, live_slot, force_cot, potential_cot):
    y = plane_rows()
    freq = np.arange(K)
    hartley_x = split_table(cas_table(freq, freq))
    factor, square = influence_factors()
    terms = np.zeros((8, K), np.float32)
    terms[:4] = factor, square, factor[y], square[y]
    params = pltpu.CompilerParams(vmem_limit_bytes=32 * 1024 * 1024)
    vmem = pl.BlockSpec(memory_space=pltpu.VMEM)
    f32 = jnp.float32
    table = pltpu.VMEM((K, ATOMS), f32)
    message = jax.ShapeDtypeStruct((2 * DEVICES, LANES), f32)
    arguments = (charge, fraction, base_cell, live_slot, force_cot, potential_cot)

    rows = pl.pallas_call(
        rows_kernel,
        out_shape=jax.ShapeDtypeStruct((K, ATOMS), jnp.int32),
        out_specs=vmem,
        compiler_params=params,
        cost_estimate=pl.CostEstimate(flops=10**9, bytes_accessed=10**6, transcendentals=0),
        name="rows",
    )()
    hartley = pl.pallas_call(
        table_kernel,
        out_shape=jax.ShapeDtypeStruct((2, K, K), jnp.bfloat16),
        in_specs=[vmem],
        out_specs=vmem,
        compiler_params=params,
        cost_estimate=pl.CostEstimate(flops=10**9, bytes_accessed=10**6, transcendentals=0),
        name="tables",
    )(rows)
    sent, spectral, atoms = pl.pallas_call(
        spread_kernel,
        out_shape=(
            message,
            jax.ShapeDtypeStruct((4, K, ATOMS), jnp.bfloat16),
            jax.ShapeDtypeStruct((SCALARS + 8, ATOMS), f32),
        ),
        in_specs=[vmem] * 8,
        out_specs=(vmem,) * 3,
        scratch_shapes=[table, table, table],
        compiler_params=params,
        name="spread",
    )(rows, *arguments, hartley)
    received = exchange(sent)
    solved = pl.pallas_call(
        plane_kernel,
        out_shape=message,
        in_specs=[vmem] * 4,
        out_specs=vmem,
        compiler_params=params,
        name="plane",
    )(received, hartley, jnp.asarray(hartley_x), jnp.asarray(terms))
    returned = exchange(solved)
    return pl.pallas_call(
        sample_kernel,
        out_shape=(
            jax.ShapeDtypeStruct((3, 1, 1, ATOMS), f32),
            jax.ShapeDtypeStruct((1, 1, ATOMS), f32),
            jax.ShapeDtypeStruct((1, 1, ATOMS), f32),
        ),
        in_specs=[vmem] * 3,
        out_specs=(vmem, vmem, vmem),
        scratch_shapes=[table, table, table],
        compiler_params=params,
        name="sample",
    )(returned, spectral, atoms)


def solution(mesh):
    return jax.shard_map(
        on_device,
        mesh=mesh,
        in_specs=(
            P("gx", "gy", None),
            P(None, "gx", "gy", None),
            P("gx", "gy", None),
            P("gx", "gy", None),
            P(None, "gx", "gy", None),
            P("gx", "gy", None),
        ),
        out_specs=(P(None, "gx", "gy", None), P("gx", "gy", None), P("gx", "gy", None)),
        check_vma=False,
    )
```

```python
import math

import jax
import jax.numpy as jnp
import ml_dtypes
import numpy as np
from jax import lax
from jax.experimental import pallas as pl
from jax.experimental.pallas import tpu as pltpu
from jax.sharding import PartitionSpec as P

K = 256
CY = 8
N_GX = 16
N_GY = 32
ATOMS = 256
DEVICES = N_GX * N_GY
LANES = 128
SCALARS = 256
HALVES = (slice(0, K // 2), slice(K // 2, K))

EWALD_SPLIT = 0.8


def cas_table(left, right):
    angles = 2.0 * math.pi / K * (left[:, None] * right[None, :] % K)
    return np.cos(angles) + np.sin(angles)


def split_table(table):
    high = table.astype(np.float32).astype(ml_dtypes.bfloat16)
    low = (table - high.astype(np.float64)).astype(np.float32).astype(ml_dtypes.bfloat16)
    return np.stack([high, low])


def plane_rows():
    m, gy = np.meshgrid(np.arange(CY), np.arange(N_GY), indexing="ij")
    return (gy * CY + m).reshape(-1)


def natural(index):
    return jnp.bitwise_or(
        jnp.left_shift(jnp.bitwise_and(index, N_GY - 1), 3), jnp.right_shift(index, 5)
    )


def influence_factors():
    freq = np.arange(K)
    nearest = np.minimum(freq, K - freq).astype(np.float64)
    damping = math.pi * math.pi / (EWALD_SPLIT * EWALD_SPLIT * K * K)
    cosine = np.cos(2.0 * math.pi / K * freq)
    factor = np.exp(-damping * nearest * nearest) * 9.0 / (2.0 + cosine) ** 2
    return factor.astype(np.float32), (nearest * nearest).astype(np.float32)


def split(value):
    high = value.astype(jnp.bfloat16)
    low = (value - high.astype(jnp.float32)).astype(jnp.bfloat16)
    return high, low


def product(left, right, dims=((1,), (0,))):
    def one(a, b):
        return lax.dot_general(a, b, (dims, ((), ())), preferred_element_type=jnp.float32)

    return one(left[0], right[0]) + (one(left[0], right[1]) + one(left[1], right[0]))


def joined(blocks):
    return tuple(jnp.concatenate(pair, axis=0) for pair in zip(*blocks))


def spline_terms(fraction):
    square = fraction * fraction
    cubic_part = square * fraction
    remain = 1.0 - fraction
    weights = (
        remain * remain * remain * (1.0 / 6.0),
        (3.0 * cubic_part - 6.0 * square + 4.0) * (1.0 / 6.0),
        (-3.0 * cubic_part + 3.0 * square + 3.0 * fraction + 1.0) * (1.0 / 6.0),
        cubic_part * (1.0 / 6.0),
    )
    slopes = (
        -0.5 * remain * remain,
        (3.0 * square - 4.0 * fraction) * 0.5,
        (-3.0 * square + 2.0 * fraction + 1.0) * 0.5,
        0.5 * square,
    )
    return weights, slopes


def banded(place, terms):
    hits = [place == offset for offset in range(4)]

    def table(values):
        out = jnp.zeros(place.shape, jnp.float32)
        for hit, value in zip(hits, values):
            out = jnp.where(hit, jnp.broadcast_to(value, place.shape), out)
        return out

    return [table(values) for values in terms]


def row_numbers(rows):
    return lax.broadcasted_iota(jnp.int32, (rows, ATOMS), 0)


SHIFT_X = 53
SHIFT_XY = 57
EDGES = {0: 8, 1: 9, 7: -1}


def halo_x(lane):
    low = (lane == 15) | (lane == 4) | (lane == 8)
    upper = (lane == 0) | (lane == 5) | (lane == 9)
    top = (lane == 1) | (lane == 6) | (lane == 10)
    return jnp.where(low, -1, jnp.where(upper, 16, jnp.where(top, 17, 99)))


def halo_y(lane, j):
    before, behind = (j - 4) % 8, (j - 3) % 8
    choice = (
        ((lane <= 1) | (lane == 15), j),
        (lane == 4, before if before in EDGES else 99),
        ((lane == 5) | (lane == 6), behind if behind in EDGES else 99),
        (lane == 8, EDGES.get(before, 99)),
        ((lane == 9) | (lane == 10), EDGES.get(behind, 99)),
    )
    out = jnp.full(lane.shape, 99, jnp.int32)
    for mask, y in choice:
        out = jnp.where(mask, y, out)
    return out


def domain_tables(cells, fraction_ref):
    cell_x = jnp.right_shift(cells, 7) - 1
    cell_y = jnp.bitwise_and(jnp.right_shift(cells, 4), CY - 1) - 1
    terms_x = spline_terms(fraction_ref[0, 0])
    terms_y = spline_terms(fraction_ref[1, 0])
    lane = row_numbers(16)
    out = banded(lane - cell_x, terms_x) + banded(halo_x(lane) - cell_x, terms_x)
    out += banded(lane - 1 - cell_y, terms_y)
    for j in range(2, 7):
        out += banded(halo_y(lane, j) - cell_y, terms_y)
    return out


def message_blocks(tables):
    wx, dx, wx_halo, dx_halo, wy, dy = tables[:6]

    def row(y):
        return wy[y + 1 : y + 2], dy[y + 1 : y + 2]

    blocks = [(wx, dx) + row(m) for m in range(CY)]
    for j in range(8):
        if j in EDGES:
            blocks.append((wx, dx) + row(EDGES[j]))
        else:
            blocks.append((wx_halo, dx_halo, tables[2 + 2 * j], tables[3 + 2 * j]))
    return blocks


def rows_kernel(rows):
    rows[...] = natural(row_numbers(K))


def table_kernel(rows, hartley):
    cell = rows[...]
    frequency = natural(lax.broadcasted_iota(jnp.int32, (K, K), 1))
    turn = jnp.bitwise_and(cell * frequency + K // 8, K - 1) - K // 2
    quarter = jnp.where(turn > K // 4, K // 2 - turn, jnp.where(turn < -K // 4, -K // 2 - turn, turn))
    angle = quarter.astype(jnp.float32) * (2.0 * math.pi / K)
    square = angle * angle
    series = jnp.full((K, K), -1.0 / math.factorial(11), jnp.float32)
    for order in (9, 7, 5, 3, 1):
        series = series * square + (-1.0) ** (order // 2) / math.factorial(order)
    high, low = split(series * angle * -math.sqrt(2.0))
    hartley[0] = high
    hartley[1] = low


def z_tables(rows, first, terms):
    zeros = [jnp.zeros((8, LANES), jnp.float32)] * 2
    halves = []
    for half in range(2):
        lanes = slice(half * LANES, (half + 1) * LANES)
        here = [[value[:, lanes] for value in values] for values in terms]

        def piece(start, count):
            place = rows[start : start + count, lanes] - first[:, lanes]
            return banded(jnp.bitwise_and(place, K - 1), here)

        pieces = []
        for m in range(CY):
            line = [piece(m * N_GY + half * 16, 16)]
            behind = piece(m * N_GY + (1 - half) * 16, 8) if m <= 2 else zeros
            before = piece(m * N_GY + (1 - half) * 16 + 8, 8) if m == 7 else zeros
            pieces += line + [behind, before] if half == 0 else [behind, before] + line
        halves.append([jnp.concatenate([part[i] for part in pieces], axis=0) for i in range(2)])
    return [jnp.concatenate([halves[0][i], halves[1][i]], axis=1) for i in range(2)]


def spread_kernel(
    rows, charge, fraction, base_cell, live_slot, force_cot, potential_cot, hartley,
    send, spectral, atoms, table_a, table_b, table_c,
):
    def store(field, value):
        for row in range(2):
            send[pl.ds(field * 2 * K + row, K, stride=2), :] = value[
                :, row * LANES : (row + 1) * LANES
            ]

    cells = base_cell[0]
    slot = lax.broadcasted_iota(jnp.int32, (1, ATOMS), 1)
    base_z = jnp.bitwise_and(slot, -16) + jnp.bitwise_and(cells, 15)
    wz, dz = z_tables(rows, base_z - 1, spline_terms(fraction[2, 0]))
    tables = domain_tables(cells, fraction)
    for index, value in enumerate(tables):
        atoms[index * 16 : (index + 1) * 16, :] = value
    live = live_slot[0].astype(jnp.float32)
    live_charge = charge[0] * live
    scalars = (live, live_charge, force_cot[0, 0], force_cot[1, 0], force_cot[2, 0])
    for row, value in enumerate(scalars):
        atoms[SCALARS + row : SCALARS + row + 1, :] = value
    atoms[SCALARS + 5 : SCALARS + 8, :] = jnp.zeros((3, ATOMS), jnp.float32)
    along_x = -live_charge * force_cot[0, 0]
    along_y = -live_charge * force_cot[1, 0]
    along_z = -live_charge * force_cot[2, 0]
    direct = live * potential_cot[0]
    for index, (wx, dx, wy, dy) in enumerate(message_blocks(tables)):
        rows = slice(index * 16, (index + 1) * 16)
        table_a[rows, :] = wx * (live_charge * wy)
        table_b[rows, :] = dx * (along_x * wy) + wx * (along_y * dy + direct * wy)
        table_c[rows, :] = wx * (along_z * wy)
    nt = ((1,), (1,))
    blocks = [(hartley[0, cut, :], hartley[1, cut, :]) for cut in HALVES]
    zw, zd = [
        joined([split(product(block, value)) for block in blocks]) for value in (split(wz), split(dz))
    ]
    for index, value in enumerate(zw + zd):
        spectral[index] = value
    store(0, product(zw, split(table_a[...]), nt))
    store(1, product(zw, split(table_b[...]), nt) + product(zd, split(table_c[...]), nt))


def transposed_blocks(values):
    values = list(values)
    block = jnp.right_shift(lax.broadcasted_iota(jnp.int32, values[0].shape, 1), 4)
    for step in (1, 2, 4):
        upper = jnp.bitwise_and(block, step) != 0
        for i in range(8):
            if i & step == 0:
                first, second = values[i], values[i + step]
                values[i] = jnp.where(upper, pltpu.roll(second, 16 * step, 1), first)
                values[i + step] = jnp.where(upper, second, pltpu.roll(first, LANES - 16 * step, 1))
    return values


def plane_kernel(received, hartley, hartley_x, terms, send):
    device = lax.axis_index("gx") * N_GY + lax.axis_index("gy")
    here = lax.broadcasted_iota(jnp.int32, (1, K), 1) == lax.rem(device, K)
    factor_x, square_x, factor_y, square_y = [terms[row : row + 1, :] for row in range(4)]
    factor_z = jnp.sum(jnp.where(here, factor_y, 0.0), axis=1, keepdims=True)
    square_z = jnp.sum(jnp.where(here, square_y, 0.0), axis=1, keepdims=True)
    hx = (hartley_x[0], hartley_x[1])
    place = lax.broadcasted_iota(jnp.int32, (N_GY, LANES), 1)
    block = jnp.right_shift(place, 4)
    lane = jnp.bitwise_and(place, 15)
    low = lane == 15
    high = lane <= 1
    last = block == 7
    first = block <= 1
    edge = last | first

    def rows(gx, half):
        return pl.ds(gx * 2 * N_GY + half, N_GY, stride=2)

    along_x, corners = [], []
    for gx in range(N_GX):
        halo = received[rows(gx, 1), :]
        along_x.append(jnp.where(edge, pltpu.roll(halo, LANES - SHIFT_X, 1), halo))
        corners.append(pltpu.roll(halo, LANES - SHIFT_XY, 1))

    def from_sides(values, gx):
        after, before = values[(gx + 1) % N_GX], values[gx - 1]
        return jnp.where(low, after, jnp.where(high, before, 0.0))

    folded = []
    for gx in range(N_GX):
        own = received[rows(gx, 0), :] + from_sides(along_x, gx)
        side = received[rows(gx, 1), :] + from_sides(corners, gx)
        after, before = pltpu.roll(side, N_GY - 1, 0), pltpu.roll(side, 1, 0)
        folded.append(own + jnp.where(last, after, jnp.where(first, before, 0.0)))
    groups = [transposed_blocks(folded[group * 8 : group * 8 + 8]) for group in range(2)]
    total_sq = jnp.transpose(square_y) + (square_x + square_z)
    factor = jnp.transpose(factor_y) * (factor_x * (factor_z * (1.0 / (math.pi * K))))
    kernel = jnp.where(total_sq > 0.0, factor / jnp.maximum(total_sq, 1.0), 0.0)
    hy = [(hartley[0, cut, :], hartley[1, cut, :]) for cut in HALVES]
    lines = [
        jnp.concatenate([jnp.concatenate(group[m : m + 4], axis=0) for group in groups], axis=1)
        for m in (0, 4)
    ]
    half_way = joined([split(product(split(line), hx)) for line in lines])
    spectrum = [product(block, half_way) * kernel[cut] for block, cut in zip(hy, HALVES)]
    spectrum = joined([split(block) for block in spectrum])
    half_way = [product(block, spectrum) for block in hy]
    solved = [product(split(block), hx) for block in half_way]
    own = []
    for group in range(2):
        lanes = slice(group * LANES, (group + 1) * LANES)
        own += transposed_blocks(
            solved[m // 4][m % 4 * N_GY : (m % 4 + 1) * N_GY, lanes] for m in range(CY)
        )
    sides = [
        jnp.where(last, pltpu.roll(value, 1, 0), pltpu.roll(value, N_GY - 1, 0)) for value in own
    ]

    def to_sides(values, gx):
        return jnp.where(low, values[gx - 1], values[(gx + 1) % N_GX])

    turned_x = (lane >= 4) & (lane <= 6)
    turned_xy = (lane >= 8) & (lane <= 10)
    for gx in range(N_GX):
        cells_x = to_sides(own, gx)
        cells_xy = to_sides(sides, gx)
        halo = jnp.where(turned_x, pltpu.roll(cells_x, SHIFT_X, 1), cells_x)
        halo = jnp.where(turned_xy, pltpu.roll(cells_xy, SHIFT_XY, 1), halo)
        send[rows(gx, 0), :] = own[gx]
        send[rows(gx, 1), :] = jnp.where(edge, sides[gx], halo)


def sample_kernel(
    received, spectral, atoms, forces, potential, charge_grad
):
    def field(index):
        halves = [received[pl.ds(index * 2 * K + half, K, stride=2), :] for half in range(2)]
        return split(jnp.concatenate(halves, axis=1).T)

    zw = (spectral[0], spectral[1])
    zd = (spectral[2], spectral[3])
    first = field(0)
    along, sloped, answered = product(first, zw), product(first, zd), product(field(1), zw)
    live, live_charge, along_x, along_y, along_z = [
        atoms[SCALARS + row : SCALARS + row + 1, :] for row in range(5)
    ]
    tables = [atoms[index * 16 : (index + 1) * 16, :] for index in range(16)]
    sums = [jnp.zeros((16, ATOMS), jnp.float32) for _ in range(5)]
    for index, (wx, dx, wy, dy) in enumerate(message_blocks(tables)):
        rows = slice(index * 16, (index + 1) * 16)
        plain = along[rows, :]
        plain_x = wx * plain
        sums[0] = sums[0] + plain_x * wy
        sums[1] = sums[1] + (dx * plain) * wy
        sums[2] = sums[2] + plain_x * dy
        sums[3] = sums[3] + (wx * sloped[rows, :]) * wy
        sums[4] = sums[4] + (wx * answered[rows, :]) * wy
    mesh_value, grad_x, grad_y, grad_z, response = [
        jnp.sum(value, axis=0, keepdims=True) for value in sums
    ]
    forces[0, 0] = -live_charge * grad_x
    forces[1, 0] = -live_charge * grad_y
    forces[2, 0] = -live_charge * grad_z
    potential[0] = live * mesh_value
    charge_grad[0] = live * (response - along_x * grad_x - along_y * grad_y - along_z * grad_z)


def exchange(blocks):
    swapped = lax.all_to_all(
        blocks.reshape(DEVICES, 2, LANES), ("gx", "gy"), split_axis=0, concat_axis=0, tiled=True
    )
    return swapped.reshape(2 * DEVICES, LANES)


def on_device(charge, fraction, base_cell, live_slot, force_cot, potential_cot):
    y = plane_rows()
    freq = np.arange(K)
    hartley_x = split_table(cas_table(freq, freq))
    factor, square = influence_factors()
    terms = np.zeros((8, K), np.float32)
    terms[:4] = factor, square, factor[y], square[y]
    params = pltpu.CompilerParams(vmem_limit_bytes=32 * 1024 * 1024)
    vmem = pl.BlockSpec(memory_space=pltpu.VMEM)
    f32 = jnp.float32
    table = pltpu.VMEM((K, ATOMS), f32)
    message = jax.ShapeDtypeStruct((2 * DEVICES, LANES), f32)
    arguments = (charge, fraction, base_cell, live_slot, force_cot, potential_cot)

    rows = pl.pallas_call(
        rows_kernel,
        out_shape=jax.ShapeDtypeStruct((K, ATOMS), jnp.int32),
        out_specs=vmem,
        compiler_params=params,
        cost_estimate=pl.CostEstimate(flops=10**9, bytes_accessed=10**6, transcendentals=0),
        name="rows",
    )()
    hartley = pl.pallas_call(
        table_kernel,
        out_shape=jax.ShapeDtypeStruct((2, K, K), jnp.bfloat16),
        in_specs=[vmem],
        out_specs=vmem,
        compiler_params=params,
        cost_estimate=pl.CostEstimate(flops=10**9, bytes_accessed=10**6, transcendentals=0),
        name="tables",
    )(rows)
    sent, spectral, atoms = pl.pallas_call(
        spread_kernel,
        out_shape=(
            message,
            jax.ShapeDtypeStruct((4, K, ATOMS), jnp.bfloat16),
            jax.ShapeDtypeStruct((SCALARS + 8, ATOMS), f32),
        ),
        in_specs=[vmem] * 8,
        out_specs=(vmem,) * 3,
        scratch_shapes=[table, table, table],
        compiler_params=params,
        name="spread",
    )(rows, *arguments, hartley)
    received = exchange(sent)
    solved = pl.pallas_call(
        plane_kernel,
        out_shape=message,
        in_specs=[vmem] * 4,
        out_specs=vmem,
        compiler_params=params,
        name="plane",
    )(received, hartley, jnp.asarray(hartley_x), jnp.asarray(terms))
    returned = exchange(solved)
    return pl.pallas_call(
        sample_kernel,
        out_shape=(
            jax.ShapeDtypeStruct((3, 1, 1, ATOMS), f32),
            jax.ShapeDtypeStruct((1, 1, ATOMS), f32),
            jax.ShapeDtypeStruct((1, 1, ATOMS), f32),
        ),
        in_specs=[vmem] * 3,
        out_specs=(vmem, vmem, vmem),
        compiler_params=params,
        name="sample",
    )(returned, spectral, atoms)


def solution(mesh):
    return jax.shard_map(
        on_device,
        mesh=mesh,
        in_specs=(
            P("gx", "gy", None),
            P(None, "gx", "gy", None),
            P("gx", "gy", None),
            P("gx", "gy", None),
            P(None, "gx", "gy", None),
            P("gx", "gy", None),
        ),
        out_specs=(P(None, "gx", "gy", None), P("gx", "gy", None), P("gx", "gy", None)),
        check_vma=False,
    )
```

```python
import math

import jax
import jax.numpy as jnp
import ml_dtypes
import numpy as np
from jax import lax
from jax.experimental import pallas as pl
from jax.experimental.pallas import tpu as pltpu
from jax.sharding import PartitionSpec as P

K = 256
CY = 8
N_GX = 16
N_GY = 32
ATOMS = 256
DEVICES = N_GX * N_GY
LANES = 128
SCALARS = 256
HALVES = (slice(0, K // 2), slice(K // 2, K))

EWALD_SPLIT = 0.8


def cas_table(left, right):
    angles = 2.0 * math.pi / K * (left[:, None] * right[None, :] % K)
    return np.cos(angles) + np.sin(angles)


def split_table(table):
    high = table.astype(np.float32).astype(ml_dtypes.bfloat16)
    low = (table - high.astype(np.float64)).astype(np.float32).astype(ml_dtypes.bfloat16)
    return np.stack([high, low])


def plane_rows():
    m, gy = np.meshgrid(np.arange(CY), np.arange(N_GY), indexing="ij")
    return (gy * CY + m).reshape(-1)


def natural(index):
    return jnp.bitwise_or(
        jnp.left_shift(jnp.bitwise_and(index, N_GY - 1), 3), jnp.right_shift(index, 5)
    )


def influence_factors():
    freq = np.arange(K)
    nearest = np.minimum(freq, K - freq).astype(np.float64)
    damping = math.pi * math.pi / (EWALD_SPLIT * EWALD_SPLIT * K * K)
    cosine = np.cos(2.0 * math.pi / K * freq)
    factor = np.exp(-damping * nearest * nearest) * 9.0 / (2.0 + cosine) ** 2
    return factor.astype(np.float32), (nearest * nearest).astype(np.float32)


def split(value):
    high = value.astype(jnp.bfloat16)
    low = (value - high.astype(jnp.float32)).astype(jnp.bfloat16)
    return high, low


def product(left, right, dims=((1,), (0,))):
    def one(a, b):
        return lax.dot_general(a, b, (dims, ((), ())), preferred_element_type=jnp.float32)

    return one(left[0], right[0]) + (one(left[0], right[1]) + one(left[1], right[0]))


def joined(blocks):
    return tuple(jnp.concatenate(pair, axis=0) for pair in zip(*blocks))


def spline_terms(fraction):
    square = fraction * fraction
    cubic_part = square * fraction
    remain = 1.0 - fraction
    weights = (
        remain * remain * remain * (1.0 / 6.0),
        (3.0 * cubic_part - 6.0 * square + 4.0) * (1.0 / 6.0),
        (-3.0 * cubic_part + 3.0 * square + 3.0 * fraction + 1.0) * (1.0 / 6.0),
        cubic_part * (1.0 / 6.0),
    )
    slopes = (
        -0.5 * remain * remain,
        (3.0 * square - 4.0 * fraction) * 0.5,
        (-3.0 * square + 2.0 * fraction + 1.0) * 0.5,
        0.5 * square,
    )
    return weights, slopes


def banded(place, terms):
    hits = [place == offset for offset in range(4)]

    def table(values):
        out = jnp.zeros(place.shape, jnp.float32)
        for hit, value in zip(hits, values):
            out = jnp.where(hit, jnp.broadcast_to(value, place.shape), out)
        return out

    return [table(values) for values in terms]


def row_numbers(rows):
    return lax.broadcasted_iota(jnp.int32, (rows, ATOMS), 0)


SHIFT_X = 53
SHIFT_XY = 57
EDGES = {0: 8, 1: 9, 7: -1}


def halo_x(lane):
    low = (lane == 15) | (lane == 4) | (lane == 8)
    upper = (lane == 0) | (lane == 5) | (lane == 9)
    top = (lane == 1) | (lane == 6) | (lane == 10)
    return jnp.where(low, -1, jnp.where(upper, 16, jnp.where(top, 17, 99)))


def halo_y(lane, j):
    before, behind = (j - 4) % 8, (j - 3) % 8
    choice = (
        ((lane <= 1) | (lane == 15), j),
        (lane == 4, before if before in EDGES else 99),
        ((lane == 5) | (lane == 6), behind if behind in EDGES else 99),
        (lane == 8, EDGES.get(before, 99)),
        ((lane == 9) | (lane == 10), EDGES.get(behind, 99)),
    )
    out = jnp.full(lane.shape, 99, jnp.int32)
    for mask, y in choice:
        out = jnp.where(mask, y, out)
    return out


def domain_tables(cells, fraction_ref, rows):
    cell_x = jnp.right_shift(cells, 7) - 1
    cell_y = jnp.bitwise_and(jnp.right_shift(cells, 4), CY - 1) - 1
    terms_x = spline_terms(fraction_ref[0, 0])
    terms_y = spline_terms(fraction_ref[1, 0])
    lane = row_numbers(16)
    out = banded(lane - cell_x, terms_x) + banded(rows[K : K + 16, :] - cell_x, terms_x)
    out += banded(lane - 1 - cell_y, terms_y)
    for j in range(2, 7):
        out += banded(rows[K + 16 * j - 16 : K + 16 * j, :] - cell_y, terms_y)
    return out


def message_blocks(tables):
    wx, dx, wx_halo, dx_halo, wy, dy = tables[:6]

    def row(y):
        return wy[y + 1 : y + 2], dy[y + 1 : y + 2]

    blocks = [(wx, dx) + row(m) for m in range(CY)]
    for j in range(8):
        if j in EDGES:
            blocks.append((wx, dx) + row(EDGES[j]))
        else:
            blocks.append((wx_halo, dx_halo, tables[2 + 2 * j], tables[3 + 2 * j]))
    return blocks


def rows_kernel(rows):
    rows[0:K, :] = natural(row_numbers(K))
    lane = row_numbers(16)
    rows[K : K + 16, :] = halo_x(lane)
    for j in range(2, 7):
        rows[K + 16 * j - 16 : K + 16 * j, :] = halo_y(lane, j)


def table_kernel(rows, hartley):
    cell = rows[0:K, :]
    frequency = natural(lax.broadcasted_iota(jnp.int32, (K, K), 1))
    turn = jnp.bitwise_and(cell * frequency + K // 8, K - 1) - K // 2
    quarter = jnp.where(turn > K // 4, K // 2 - turn, jnp.where(turn < -K // 4, -K // 2 - turn, turn))
    angle = quarter.astype(jnp.float32) * (2.0 * math.pi / K)
    square = angle * angle
    series = jnp.full((K, K), -1.0 / math.factorial(11), jnp.float32)
    for order in (9, 7, 5, 3, 1):
        series = series * square + (-1.0) ** (order // 2) / math.factorial(order)
    high, low = split(series * angle * -math.sqrt(2.0))
    hartley[0] = high
    hartley[1] = low


def z_tables(rows, first, terms):
    zeros = [jnp.zeros((8, LANES), jnp.float32)] * 2
    halves = []
    for half in range(2):
        lanes = slice(half * LANES, (half + 1) * LANES)
        here = [[value[:, lanes] for value in values] for values in terms]

        def piece(start, count):
            place = rows[start : start + count, lanes] - first[:, lanes]
            return banded(jnp.bitwise_and(place, K - 1), here)

        pieces = []
        for m in range(CY):
            line = [piece(m * N_GY + half * 16, 16)]
            behind = piece(m * N_GY + (1 - half) * 16, 8) if m <= 2 else zeros
            before = piece(m * N_GY + (1 - half) * 16 + 8, 8) if m == 7 else zeros
            pieces += line + [behind, before] if half == 0 else [behind, before] + line
        halves.append([jnp.concatenate([part[i] for part in pieces], axis=0) for i in range(2)])
    return [jnp.concatenate([halves[0][i], halves[1][i]], axis=1) for i in range(2)]


def spread_kernel(
    rows, charge, fraction, base_cell, live_slot, force_cot, potential_cot, hartley,
    send, spectral, atoms, table_a, table_b, table_c,
):
    def store(field, value):
        for row in range(2):
            send[pl.ds(field * 2 * K + row, K, stride=2), :] = value[
                :, row * LANES : (row + 1) * LANES
            ]

    cells = base_cell[0]
    slot = lax.broadcasted_iota(jnp.int32, (1, ATOMS), 1)
    base_z = jnp.bitwise_and(slot, -16) + jnp.bitwise_and(cells, 15)
    wz, dz = z_tables(rows, base_z - 1, spline_terms(fraction[2, 0]))
    tables = domain_tables(cells, fraction, rows)
    for index, value in enumerate(tables):
        atoms[index * 16 : (index + 1) * 16, :] = value
    live = live_slot[0].astype(jnp.float32)
    live_charge = charge[0] * live
    scalars = (live, live_charge, force_cot[0, 0], force_cot[1, 0], force_cot[2, 0])
    for row, value in enumerate(scalars):
        atoms[SCALARS + row : SCALARS + row + 1, :] = value
    atoms[SCALARS + 5 : SCALARS + 8, :] = jnp.zeros((3, ATOMS), jnp.float32)
    along_x = -live_charge * force_cot[0, 0]
    along_y = -live_charge * force_cot[1, 0]
    along_z = -live_charge * force_cot[2, 0]
    direct = live * potential_cot[0]
    for index, (wx, dx, wy, dy) in enumerate(message_blocks(tables)):
        rows = slice(index * 16, (index + 1) * 16)
        table_a[rows, :] = wx * (live_charge * wy)
        table_b[rows, :] = dx * (along_x * wy) + wx * (along_y * dy + direct * wy)
        table_c[rows, :] = wx * (along_z * wy)
    nt = ((1,), (1,))
    blocks = [(hartley[0, cut, :], hartley[1, cut, :]) for cut in HALVES]
    zw, zd = [
        joined([split(product(block, value)) for block in blocks]) for value in (split(wz), split(dz))
    ]
    for index, value in enumerate(zw + zd):
        spectral[index] = value
    store(0, product(zw, split(table_a[...]), nt))
    store(1, product(zw, split(table_b[...]), nt) + product(zd, split(table_c[...]), nt))


def exchanged(values, steps, members):
    block = jnp.right_shift(lax.broadcasted_iota(jnp.int32, values[members[0]].shape, 1), 4)
    for step in steps:
        upper = jnp.bitwise_and(block, step) != 0
        for i in members:
            if i & step == 0:
                first, second = values[i], values[i + step]
                values[i] = jnp.where(upper, pltpu.roll(second, 16 * step, 1), first)
                values[i + step] = jnp.where(upper, second, pltpu.roll(first, LANES - 16 * step, 1))


def transposed_blocks(values):
    values = list(values)
    exchanged(values, (1, 2, 4), range(8))
    return values


def plane_kernel(received, hartley, hartley_x, terms, send):
    device = lax.axis_index("gx") * N_GY + lax.axis_index("gy")
    here = lax.broadcasted_iota(jnp.int32, (1, K), 1) == lax.rem(device, K)
    factor_x, square_x, factor_y, square_y = [terms[row : row + 1, :] for row in range(4)]
    factor_z = jnp.sum(jnp.where(here, factor_y, 0.0), axis=1, keepdims=True)
    square_z = jnp.sum(jnp.where(here, square_y, 0.0), axis=1, keepdims=True)
    hx = (hartley_x[0], hartley_x[1])
    place = lax.broadcasted_iota(jnp.int32, (N_GY, LANES), 1)
    block = jnp.right_shift(place, 4)
    lane = jnp.bitwise_and(place, 15)
    low = lane == 15
    high = lane <= 1
    last = block == 7
    first = block <= 1
    edge = last | first

    def rows(gx, half):
        return pl.ds(gx * 2 * N_GY + half, N_GY, stride=2)

    along_x, corners = [], []
    for gx in range(N_GX):
        halo = received[rows(gx, 1), :]
        along_x.append(jnp.where(edge, pltpu.roll(halo, LANES - SHIFT_X, 1), halo))
        corners.append(pltpu.roll(halo, LANES - SHIFT_XY, 1))

    def from_sides(values, gx):
        after, before = values[(gx + 1) % N_GX], values[gx - 1]
        return jnp.where(low, after, jnp.where(high, before, 0.0))

    folded = []
    for gx in range(N_GX):
        own = received[rows(gx, 0), :] + from_sides(along_x, gx)
        side = received[rows(gx, 1), :] + from_sides(corners, gx)
        after, before = pltpu.roll(side, N_GY - 1, 0), pltpu.roll(side, 1, 0)
        folded.append(own + jnp.where(last, after, jnp.where(first, before, 0.0)))
    total_sq = jnp.transpose(square_y) + (square_x + square_z)
    factor = jnp.transpose(factor_y) * (factor_x * (factor_z * (1.0 / (math.pi * K))))
    kernel = jnp.where(total_sq > 0.0, factor / jnp.maximum(total_sq, 1.0), 0.0)
    hy = [(hartley[0, cut, :], hartley[1, cut, :]) for cut in HALVES]
    groups = [folded[0:8], folded[8:16]]
    for group in groups:
        exchanged(group, (4,), range(8))
    lines = []
    for low_line in (0, 4):
        members = range(low_line, low_line + 4)
        for group in groups:
            exchanged(group, (2, 1), members)
        line = [jnp.concatenate([group[m] for m in members], axis=0) for group in groups]
        lines.append(split(product(split(jnp.concatenate(line, axis=1)), hx)))
    half_way = joined(lines)
    spectrum = [product(block, half_way) * kernel[cut] for block, cut in zip(hy, HALVES)]
    spectrum = joined([split(block) for block in spectrum])
    half_way = [product(block, spectrum) for block in hy]
    solved = [product(split(block), hx) for block in half_way]
    own = []
    for group in range(2):
        lanes = slice(group * LANES, (group + 1) * LANES)
        own += transposed_blocks(
            solved[m // 4][m % 4 * N_GY : (m % 4 + 1) * N_GY, lanes] for m in range(CY)
        )
    sides = [
        jnp.where(last, pltpu.roll(value, 1, 0), pltpu.roll(value, N_GY - 1, 0)) for value in own
    ]

    def to_sides(values, gx):
        return jnp.where(low, values[gx - 1], values[(gx + 1) % N_GX])

    turned_x = (lane >= 4) & (lane <= 6)
    turned_xy = (lane >= 8) & (lane <= 10)
    for gx in range(N_GX):
        cells_x = to_sides(own, gx)
        cells_xy = to_sides(sides, gx)
        halo = jnp.where(turned_x, pltpu.roll(cells_x, SHIFT_X, 1), cells_x)
        halo = jnp.where(turned_xy, pltpu.roll(cells_xy, SHIFT_XY, 1), halo)
        send[rows(gx, 0), :] = own[gx]
        send[rows(gx, 1), :] = jnp.where(edge, sides[gx], halo)


def sample_kernel(
    received, spectral, atoms, forces, potential, charge_grad, sample_a, sample_b, sample_c
):
    def field(index):
        halves = [received[pl.ds(index * 2 * K + half, K, stride=2), :] for half in range(2)]
        return split(jnp.concatenate(halves, axis=1).T)

    zw = (spectral[0], spectral[1])
    zd = (spectral[2], spectral[3])
    first = field(0)
    sample_a[...] = product(first, zw)
    sample_b[...] = product(first, zd)
    sample_c[...] = product(field(1), zw)
    live, live_charge, along_x, along_y, along_z = [
        atoms[SCALARS + row : SCALARS + row + 1, :] for row in range(5)
    ]
    tables = [atoms[index * 16 : (index + 1) * 16, :] for index in range(16)]
    sums = [jnp.zeros((16, ATOMS), jnp.float32) for _ in range(5)]
    for index, (wx, dx, wy, dy) in enumerate(message_blocks(tables)):
        rows = slice(index * 16, (index + 1) * 16)
        plain = sample_a[rows, :]
        plain_x = wx * plain
        sums[0] = sums[0] + plain_x * wy
        sums[1] = sums[1] + (dx * plain) * wy
        sums[2] = sums[2] + plain_x * dy
        sums[3] = sums[3] + (wx * sample_b[rows, :]) * wy
        sums[4] = sums[4] + (wx * sample_c[rows, :]) * wy
    mesh_value, grad_x, grad_y, grad_z, response = [
        jnp.sum(value, axis=0, keepdims=True) for value in sums
    ]
    forces[0, 0] = -live_charge * grad_x
    forces[1, 0] = -live_charge * grad_y
    forces[2, 0] = -live_charge * grad_z
    potential[0] = live * mesh_value
    charge_grad[0] = live * (response - along_x * grad_x - along_y * grad_y - along_z * grad_z)


def exchange(blocks):
    swapped = lax.all_to_all(
        blocks.reshape(DEVICES, 2, LANES), ("gx", "gy"), split_axis=0, concat_axis=0, tiled=True
    )
    return swapped.reshape(2 * DEVICES, LANES)


def on_device(charge, fraction, base_cell, live_slot, force_cot, potential_cot):
    y = plane_rows()
    freq = np.arange(K)
    hartley_x = split_table(cas_table(freq, freq))
    factor, square = influence_factors()
    terms = np.zeros((8, K), np.float32)
    terms[:4] = factor, square, factor[y], square[y]
    params = pltpu.CompilerParams(vmem_limit_bytes=32 * 1024 * 1024)
    vmem = pl.BlockSpec(memory_space=pltpu.VMEM)
    f32 = jnp.float32
    table = pltpu.VMEM((K, ATOMS), f32)
    message = jax.ShapeDtypeStruct((2 * DEVICES, LANES), f32)
    arguments = (charge, fraction, base_cell, live_slot, force_cot, potential_cot)

    rows = pl.pallas_call(
        rows_kernel,
        out_shape=jax.ShapeDtypeStruct((K + 96, ATOMS), jnp.int32),
        out_specs=vmem,
        compiler_params=params,
        cost_estimate=pl.CostEstimate(flops=10**9, bytes_accessed=10**6, transcendentals=0),
        name="rows",
    )()
    hartley = pl.pallas_call(
        table_kernel,
        out_shape=jax.ShapeDtypeStruct((2, K, K), jnp.bfloat16),
        in_specs=[vmem],
        out_specs=vmem,
        compiler_params=params,
        cost_estimate=pl.CostEstimate(flops=10**9, bytes_accessed=10**6, transcendentals=0),
        name="tables",
    )(rows)
    sent, spectral, atoms = pl.pallas_call(
        spread_kernel,
        out_shape=(
            message,
            jax.ShapeDtypeStruct((4, K, ATOMS), jnp.bfloat16),
            jax.ShapeDtypeStruct((SCALARS + 8, ATOMS), f32),
        ),
        in_specs=[vmem] * 8,
        out_specs=(vmem,) * 3,
        scratch_shapes=[table, table, table],
        compiler_params=params,
        name="spread",
    )(rows, *arguments, hartley)
    received = exchange(sent)
    solved = pl.pallas_call(
        plane_kernel,
        out_shape=message,
        in_specs=[vmem] * 4,
        out_specs=vmem,
        compiler_params=params,
        name="plane",
    )(received, hartley, jnp.asarray(hartley_x), jnp.asarray(terms))
    returned = exchange(solved)
    return pl.pallas_call(
        sample_kernel,
        out_shape=(
            jax.ShapeDtypeStruct((3, 1, 1, ATOMS), f32),
            jax.ShapeDtypeStruct((1, 1, ATOMS), f32),
            jax.ShapeDtypeStruct((1, 1, ATOMS), f32),
        ),
        in_specs=[vmem] * 3,
        out_specs=(vmem, vmem, vmem),
        scratch_shapes=[table, table, table],
        compiler_params=params,
        name="sample",
    )(returned, spectral, atoms)


def solution(mesh):
    return jax.shard_map(
        on_device,
        mesh=mesh,
        in_specs=(
            P("gx", "gy", None),
            P(None, "gx", "gy", None),
            P("gx", "gy", None),
            P("gx", "gy", None),
            P(None, "gx", "gy", None),
            P("gx", "gy", None),
        ),
        out_specs=(P(None, "gx", "gy", None), P("gx", "gy", None), P("gx", "gy", None)),
        check_vma=False,
    )
```
